256 devices in a mesh: ctx: 64 (over x, z, core), tp: 4 (over y).
Axes of the slice: x: 4, y: 4, z: 8, core: 2. Of those that a mesh axis runs over, the one named last changes fastest.
Arguments:
- block_query: bfloat16 [4096, 8192], P('ctx', 'tp'), may hold values from -10 to 10
- block_key: bfloat16 [4096, 1024], P('ctx', 'tp'), may hold values from -10 to 10
- block_value: bfloat16 [4096, 1024], P('ctx', 'tp'), may hold values from -6 to 6
- question_query: bfloat16 [256, 8192], P('ctx', 'tp'), may hold values from -10 to 10
- question_key: bfloat16 [256, 1024], P('ctx', 'tp'), may hold values from -10 to 10
- question_value: bfloat16 [256, 1024], P('ctx', 'tp'), may hold values from -6 to 6
- block_fill: int32 [64], replicated, may hold values from 1 to 64, 2560 in all
Outputs:
- block_output: bfloat16 [4096, 8192], P('ctx', 'tp')
- question_output: bfloat16 [256, 8192], P(('ctx', 'tp'))
The draws below stay inside these ranges and needn't reach their ends.
Inputs may be any that keep to these rules, and one draw needn't show every extreme that they name: Block d's first block_fill[d] tokens are real, the rest padding.
All inputs are finite; a program needn't handle non-finite values.
Results may differ from the reference program's by a relative error of at most 0.0065.
Values may be sent and summed in bfloat16 or wider, within the bound.
No kernel may reach another device: no remote copies, remote signals or barrier semaphores. Data moves between devices by JAX's collectives and lax.ppermute only.
A program may use at most 256 MiB of HBM per device.

```python
import math
import jax
import jax.numpy as jnp
import numpy as np
from jax import lax

NH = 64
KV_HEADS = 8
HEAD = 128
BLOCK = 64
QTOK = 4
CONTEXT = 4096
QLEN = 256
N_CTX = 64


def draw_block_query(key, part):
    key = jax.random.fold_in(key, 31)
    return jnp.clip(1.7 * jax.random.normal(key, (CONTEXT, NH * HEAD), jnp.float32), -10.0, 10.0).astype(jnp.bfloat16)


def draw_block_key(key, part):
    key = jax.random.fold_in(key, 37)
    return jnp.clip(1.7 * jax.random.normal(key, (CONTEXT, KV_HEADS * HEAD), jnp.float32), -10.0, 10.0).astype(jnp.bfloat16)


def draw_question_query(key, part):
    key = jax.random.fold_in(key, 41)
    return jnp.clip(1.7 * jax.random.normal(key, (QLEN, NH * HEAD), jnp.float32), -10.0, 10.0).astype(jnp.bfloat16)


def draw_question_key(key, part):
    key = jax.random.fold_in(key, 43)
    return jnp.clip(1.7 * jax.random.normal(key, (QLEN, KV_HEADS * HEAD), jnp.float32), -10.0, 10.0).astype(jnp.bfloat16)


def level_of(stream_key, dims, split, low, largest):
    loudness = 1.0
    for dim, shards_of in split:
        heights = jax.random.uniform(jax.random.fold_in(jax.random.fold_in(stream_key, 6), dim), (shards_of,), jnp.float32, low / len(split), largest / len(split))
        loudness = loudness * jnp.repeat(jnp.exp(heights), dims[dim] // shards_of).reshape((-1,) + (1,) * (len(dims) - 1 - dim))
    return loudness


def length_profile(count, total, limit, lean):
    weights = [(1 << 20) // math.isqrt(grade ** lean) + 1 for grade in range(2, count + 1)]
    spare, counts = total - limit - (count - 1), [1] * (count - 1)
    while spare > 0:
        candidates = [i for i in range(count - 1) if counts[i] < limit]
        whole, budget = sum([weights[i] for i in candidates]), spare
        for i in candidates:
            more = min(limit - counts[i], max(1, budget * weights[i] // whole), spare)
            counts[i] = counts[i] + more
            spare = spare - more
    return np.array([limit] + counts)


def ragged_sizes(key, number_of, total, most, slope):
    if number_of == 2:
        one = jax.random.randint(key, (), max(1, total - most), min(most, total - 1) + 1)
        return jnp.stack([one, total - one])
    lengths = jnp.asarray(length_profile(number_of, total, most, slope), jnp.int32)
    pairs = (number_of - 1) // 2
    giver, taker = lengths[1:1 + 2 * pairs:2], lengths[2:2 + 2 * pairs:2]
    margin = jnp.minimum(giver - 1, most - taker)
    moved = jax.random.randint(jax.random.fold_in(key, 1), (pairs,), 0, 1 << 20) % (margin + 1)
    lengths = lengths.at[1:1 + 2 * pairs:2].set(giver - moved).at[2:2 + 2 * pairs:2].set(taker + moved)
    return lengths[jax.random.permutation(jax.random.fold_in(key, 2), number_of)]


def normal_values(own_key, extent, scale, limit, pieces=(), kind=jnp.bfloat16):
    gain = level_of(own_key, extent, pieces, -0.22, 0.18) if pieces else 1.0
    array = jax.random.normal(own_key, extent, jnp.float32) * scale * gain
    return jnp.minimum(jnp.maximum(array, -limit), limit).astype(kind)


def setup_inputs(seed: int = 0) -> dict:
    splits = jax.random.split(jax.random.key(seed), 8)
    return {
        "block_query": draw_block_query(jax.random.fold_in(splits[7], 71), 0),
        "block_key": draw_block_key(jax.random.fold_in(splits[7], 71), 0),
        "block_value": normal_values(splits[2], (CONTEXT, KV_HEADS * HEAD), 1.0, 6.0, ((0, 64), (1, 4))),
        "question_query": draw_question_query(jax.random.fold_in(splits[7], 71), 0),
        "question_key": draw_question_key(jax.random.fold_in(splits[7], 71), 0),
        "question_value": normal_values(splits[5], (QLEN, KV_HEADS * HEAD), 1.0, 6.0, ((0, 64), (1, 4))),
        "block_fill": ragged_sizes(splits[6], N_CTX, N_CTX * BLOCK * 5 // 8, BLOCK, 2).astype(jnp.int32),
    }


def masked_parts(scores, allowed):
    masked = jnp.where(allowed, scores, -jnp.inf)
    peak = jnp.max(masked, axis=-1, keepdims=True)
    weights = jnp.exp(masked - peak).astype(jnp.bfloat16)
    totals = jnp.sum(weights.astype(jnp.float32), axis=-1, keepdims=True)
    return peak, weights, totals


def reference(block_query, block_key, block_value, question_query, question_key, question_value, block_fill):
    groups = NH // KV_HEADS
    factor = HEAD ** -0.5
    queries = block_query.reshape(N_CTX, BLOCK, KV_HEADS, groups, HEAD)
    keys = block_key.reshape(N_CTX, BLOCK, KV_HEADS, HEAD)
    values = block_value.reshape(N_CTX, BLOCK, KV_HEADS, HEAD)
    row_ids = jnp.arange(BLOCK, dtype=jnp.int32)[:, None]
    col_ids = jnp.arange(2 * BLOCK, dtype=jnp.int32)[None, :]
    own_cols = col_ids - BLOCK

    def first_block(block):
        key_rows = jnp.concatenate([keys[0], keys[block]], 0)
        value_rows = jnp.concatenate([values[0], values[block]], 0)
        scores = jnp.einsum("ikgd,jkd->kgij", queries[block].astype(jnp.float32), key_rows.astype(jnp.float32)) * factor
        allowed = jnp.where(col_ids < BLOCK, (col_ids < block_fill[0]) & (block > 0), (own_cols <= row_ids) & (own_cols < block_fill[block]))
        peak, weights, totals = masked_parts(scores, allowed)
        mixed = jnp.einsum("kgij,jkd->kgid", weights.astype(jnp.float32), value_rows.astype(jnp.float32)) / totals
        mixed = jnp.transpose(mixed, (2, 0, 1, 3)).reshape(BLOCK, NH * HEAD)
        mixed = jnp.where(row_ids < block_fill[block], mixed, 0.0)
        return mixed.astype(jnp.bfloat16)

    block_output = lax.map(first_block, jnp.arange(N_CTX, dtype=jnp.int32)).reshape(CONTEXT, NH * HEAD)

    question_rows = question_query.reshape(QLEN, KV_HEADS, groups, HEAD).astype(jnp.float32)
    asked_keys = question_key.reshape(N_CTX, QTOK, KV_HEADS, HEAD)
    asked_values = question_value.reshape(N_CTX, QTOK, KV_HEADS, HEAD)
    query_ids = jnp.arange(QLEN, dtype=jnp.int32)[:, None]
    key_cols = jnp.arange(BLOCK + QTOK, dtype=jnp.int32)[None, :]

    def second_block(carry, block):
        run_peak, run_totals, run_sums = carry
        key_rows = jnp.concatenate([keys[block], asked_keys[block]], 0)
        value_rows = jnp.concatenate([values[block], asked_values[block]], 0)
        scores = jnp.einsum("ikgd,jkd->kgij", question_rows, key_rows.astype(jnp.float32)) * factor
        allowed = jnp.where(key_cols < BLOCK, key_cols < block_fill[block], block * QTOK + key_cols - BLOCK <= query_ids)
        peak, weights, totals = masked_parts(scores, allowed)
        sums = jnp.einsum("kgij,jkd->kgid", weights.astype(jnp.float32), value_rows.astype(jnp.float32))
        new_peak = jnp.maximum(run_peak, peak)
        old_scale = jnp.exp(run_peak - new_peak)
        new_scale = jnp.exp(peak - new_peak)
        return (new_peak, run_totals * old_scale + totals * new_scale, run_sums * old_scale + sums * new_scale), None

    start = (jnp.full((KV_HEADS, groups, QLEN, 1), -1e30, jnp.float32),
             jnp.zeros((KV_HEADS, groups, QLEN, 1), jnp.float32),
             jnp.zeros((KV_HEADS, groups, QLEN, HEAD), jnp.float32))
    final, unused = lax.scan(second_block, start, jnp.arange(N_CTX, dtype=jnp.int32))
    merged = final[2] / final[1]
    question_output = jnp.transpose(merged, (2, 0, 1, 3)).reshape(QLEN, NH * HEAD).astype(jnp.bfloat16)
    return block_output, question_output
```

```python
import functools

import jax
import jax.numpy as jnp
from jax import lax
from jax.experimental import pallas as pl
from jax.experimental.pallas import tpu as pltpu
from jax.sharding import Mesh, PartitionSpec as P

NH = 64
KV_HEADS = 8
HEAD = 128
GROUPS = NH // KV_HEADS
BLOCK = 64
QTOK = 4
NX, NZ, NC, NT = 4, 8, 2, 4
HEADS = NH // NT
KVS = KV_HEADS // NT
UNIT = 144
SCALE = HEAD**-0.5
NEG = float("-inf")
Z_OFFSETS = (0, -1, -2, -3, -4, 1, 2, 3)
X_SHIFTS = (0, 1, 3, 2)

VMEM = pl.BlockSpec(memory_space=pltpu.VMEM)
SMEM = pl.BlockSpec(memory_space=pltpu.SMEM)
PARAMS = pltpu.CompilerParams(vmem_limit_bytes=32 * 1024 * 1024)


def transpose_dot(left, right):
    return lax.dot_general(
        left, right, (((1,), (1,)), ((), ())), preferred_element_type=jnp.float32
    )


def prepare_kernel(query_ref, key_ref, value_ref, ask_key_ref, ask_value_ref, unit_ref, rows_ref):
    unit_ref[0:BLOCK, :] = key_ref[...]
    unit_ref[BLOCK : 2 * BLOCK, :] = value_ref[...]
    gap = jnp.zeros((8 - QTOK, KVS * HEAD), jnp.float32)
    tail = jnp.concatenate(
        [ask_key_ref[...].astype(jnp.float32), gap, ask_value_ref[...].astype(jnp.float32), gap], 0
    )
    unit_ref[2 * BLOCK : UNIT, :] = tail.astype(jnp.bfloat16)
    query = query_ref[...].astype(jnp.float32)
    for row in range(QTOK):
        heads = [query[row : row + 1, h * HEAD : (h + 1) * HEAD] for h in range(HEADS)]
        rows_ref[row] = jnp.concatenate(heads, 0).astype(jnp.bfloat16)


def question_kernel(
    place_ref, fill_ref, q0_ref, q1_ref, q2_ref, q3_ref, near_ref, far_ref, out_ref
):
    x, z, core = place_ref[0], place_ref[1], place_ref[2]
    units = [
        x * (NZ * NC) + lax.rem(z + offset + NZ, NZ) * NC + c
        for c in (core, 1 - core)
        for offset in Z_OFFSETS
    ]
    owners = [lax.rem(x - shift + NX, NX) for shift in X_SHIFTS]
    count = len(units)

    lane = lax.broadcasted_iota(jnp.int32, (1, count * BLOCK), 1)
    fills = jnp.zeros_like(lane)
    for n, unit in enumerate(units):
        fills = jnp.where(lane // BLOCK == n, fill_ref[unit], fills)
    bias = jnp.where(lane % BLOCK < fills, 0.0, NEG)

    lane = lax.broadcasted_iota(jnp.int32, (1, count * 8), 1)
    key_ids = jnp.zeros_like(lane)
    for n, unit in enumerate(units):
        key_ids = jnp.where(lane // 8 == n, unit * QTOK, key_ids)
    key_ids = jnp.where(lane % 8 < QTOK, key_ids + lane % 8, 1 << 20)
    rows = NX * QTOK * GROUPS
    row = lax.broadcasted_iota(jnp.int32, (rows, 1), 0)
    row_ids = (row // GROUPS) % QTOK
    for n, owner in enumerate(owners):
        first = (owner * (NZ * NC) + z * NC + core) * QTOK
        row_ids = jnp.where(row // (QTOK * GROUPS) == n, first + row_ids, row_ids)
    seen = key_ids <= row_ids

    queries = jnp.concatenate([r[...] for r in (q0_ref, q1_ref, q2_ref, q3_ref)], 0)
    queries = queries.astype(jnp.float32)
    outs, peaks, sums = [], [], []
    for kv in range(KVS):
        cols = slice(kv * HEAD, (kv + 1) * HEAD)
        q = queries[:, kv * GROUPS : (kv + 1) * GROUPS, :].reshape(rows, HEAD).astype(jnp.bfloat16)
        keys = [r[:, 0:BLOCK, cols].reshape(NZ * BLOCK, HEAD) for r in (near_ref, far_ref)]
        values = [r[:, BLOCK : 2 * BLOCK, cols].reshape(NZ * BLOCK, HEAD) for r in (near_ref, far_ref)]
        tails = [r[:, 2 * BLOCK : UNIT, cols].astype(jnp.float32) for r in (near_ref, far_ref)]
        tail_keys = jnp.concatenate([t[:, 0:8].reshape(NZ * 8, HEAD) for t in tails], 0)
        tail_values = jnp.concatenate([t[:, 8:16].reshape(NZ * 8, HEAD) for t in tails], 0)
        keys = jnp.concatenate(keys, 0)
        values = jnp.concatenate(values, 0)
        scores = transpose_dot(q, keys) * SCALE + bias
        tail = transpose_dot(q, tail_keys.astype(jnp.bfloat16)) * SCALE
        tail = jnp.where(seen, tail, NEG)
        peak = jnp.maximum(
            jnp.max(scores, axis=1, keepdims=True), jnp.max(tail, axis=1, keepdims=True)
        )
        peak = peak.astype(jnp.bfloat16).astype(jnp.float32)
        weights = jnp.exp(scores - peak).astype(jnp.bfloat16)
        tail_weights = jnp.exp(tail - peak).astype(jnp.bfloat16)
        total = jnp.sum(weights.astype(jnp.float32), axis=1, keepdims=True) + jnp.sum(
            tail_weights.astype(jnp.float32), axis=1, keepdims=True
        )
        mixed = jnp.dot(weights, values, preferred_element_type=jnp.float32) + jnp.dot(
            tail_weights, tail_values.astype(jnp.bfloat16), preferred_element_type=jnp.float32
        )
        shape = (NX * QTOK, GROUPS, HEAD)
        outs.append(mixed.reshape(shape))
        peaks.append(jnp.broadcast_to(peak, (rows, HEAD)).reshape(shape))
        sums.append(jnp.broadcast_to(total, (rows, HEAD)).reshape(shape))
    out = jnp.concatenate(outs, 1).astype(jnp.bfloat16)
    peak = jnp.concatenate(peaks, 1)
    total = jnp.concatenate(sums, 1)
    high = total.astype(jnp.bfloat16).astype(jnp.float32)
    lane = lax.broadcasted_iota(jnp.int32, peak.shape, 2)
    stats = jnp.where(lane == 0, peak, jnp.where(lane == 1, high, jnp.where(lane == 2, total - high, 0.0)))
    stats = stats.astype(jnp.bfloat16)
    for n, owner in enumerate(owners):
        target = pl.ds(owner * QTOK, QTOK)
        out_ref[target, 0:HEADS, :] = out[n * QTOK : (n + 1) * QTOK]
        out_ref[target, HEADS : 2 * HEADS, :] = stats[n * QTOK : (n + 1) * QTOK]


def merge_kernel(parts_ref, out_ref):
    sums = parts_ref[:, 0:HEADS, :].astype(jnp.float32)
    stats = parts_ref[:, HEADS : 2 * HEADS, :].astype(jnp.float32)
    peaks = stats[:, :, 0:1]
    totals = stats[:, :, 1:2] + stats[:, :, 2:3]
    parts = [slice(x * NT, (x + 1) * NT) for x in range(NX)]
    top = functools.reduce(jnp.maximum, [peaks[p] for p in parts])
    scales = [jnp.exp(peaks[p] - top) for p in parts]
    num = sum(sums[p] * s for p, s in zip(parts, scales))
    den = sum(totals[p] * s for p, s in zip(parts, scales))
    result = num / den
    for t in range(NT):
        for h in range(HEADS):
            at = (t * HEADS + h) * HEAD
            out_ref[:, at : at + HEAD] = result[t, h : h + 1, :].astype(jnp.bfloat16)


def block_kernel(
    place_ref, fill_ref, query_ref, unit_ref, a0_ref, a1_ref, a2_ref, a3_ref, out_ref, anchor_ref
):
    x, z, core = place_ref[0], place_ref[1], place_ref[2]
    device = x * (NZ * NC) + z * NC + core
    for n, ref in enumerate((a0_ref, a1_ref, a2_ref, a3_ref)):

        @pl.when(x == n)
        def _():
            anchor_ref[...] = ref[...]

    row = lax.broadcasted_iota(jnp.int32, (BLOCK, 2 * BLOCK), 0)
    col = lax.broadcasted_iota(jnp.int32, (BLOCK, 2 * BLOCK), 1)
    own = col - BLOCK
    own_fill = fill_ref[device]
    anchor_fill = jnp.where(device > 0, fill_ref[0], 0)
    limit = jnp.where(col < BLOCK, anchor_fill, own_fill + BLOCK)
    allowed = (col < limit) & (own <= row)
    keep = lax.broadcasted_iota(jnp.int32, (BLOCK, 1), 0) < own_fill
    for kv in range(KVS):
        cols = slice(kv * HEAD, (kv + 1) * HEAD)
        keys = jnp.concatenate([anchor_ref[0:BLOCK, cols], unit_ref[0:BLOCK, cols]], 0)
        values = jnp.concatenate(
            [anchor_ref[BLOCK : 2 * BLOCK, cols], unit_ref[BLOCK : 2 * BLOCK, cols]], 0
        )
        heads = range(kv * GROUPS, (kv + 1) * GROUPS)
        q = jnp.concatenate([query_ref[:, h * HEAD : (h + 1) * HEAD] for h in heads], 0)
        scores = transpose_dot(q, keys) * SCALE
        scores = scores.reshape(GROUPS, BLOCK, 2 * BLOCK)
        scores = jnp.where(allowed[None], scores, NEG)
        peak = jnp.max(scores, axis=2, keepdims=True)
        weights = jnp.exp(scores - peak).astype(jnp.bfloat16)
        total = jnp.sum(weights.astype(jnp.float32), axis=2, keepdims=True)
        mixed = jnp.dot(
            weights.reshape(GROUPS * BLOCK, 2 * BLOCK), values, preferred_element_type=jnp.float32
        )
        mixed = mixed.reshape(GROUPS, BLOCK, HEAD) / total
        mixed = jnp.where(keep[None], mixed, 0.0).astype(jnp.bfloat16)
        for n, h in enumerate(heads):
            out_ref[:, h * HEAD : (h + 1) * HEAD] = mixed[n]


def shifted(array, axis, size, shift):
    return lax.ppermute(array, axis, [(i, (i + shift) % size) for i in range(size)])


def per_device(
    block_query, block_key, block_value, question_query, question_key, question_value, block_fill
):
    bf16 = jnp.bfloat16
    x, z, core = lax.axis_index("x"), lax.axis_index("z"), lax.axis_index("core")
    place = jnp.stack([x, z, core]).astype(jnp.int32)

    unit, asked = pl.pallas_call(
        prepare_kernel,
        out_shape=(
            jax.ShapeDtypeStruct((UNIT, KVS * HEAD), bf16),
            jax.ShapeDtypeStruct((QTOK, HEADS, HEAD), bf16),
        ),
        in_specs=[VMEM] * 5,
        out_specs=(VMEM, VMEM),
        compiler_params=PARAMS,
        name="prepare",
    )(question_query, block_key, block_value, question_key, question_value)

    up = down = unit
    ups, downs = [], []
    for step in range(1, NZ // 2 + 1):
        up = shifted(up, "z", NZ, 1)
        ups.append(up)
        if step < NZ // 2:
            down = shifted(down, "z", NZ, NZ - 1)
            downs.append(down)
    others = [shifted(asked, "x", NX, s) for s in X_SHIFTS[1:]]
    near = jnp.stack([unit] + ups + downs)
    far = lax.ppermute(near, "core", [(0, 1), (1, 0)])

    offset = lax.rem(NZ - z, NZ)
    index = jnp.where(z <= NZ // 2, z, NZ // 2 + offset)
    first = lax.dynamic_index_in_dim(
        jnp.where(core == 0, near[:, : 2 * BLOCK], far[:, : 2 * BLOCK]), index, 0, keepdims=False
    )
    anchor1 = lax.ppermute(first, "x", [(0, 1)])
    anchor3 = lax.ppermute(first, "x", [(0, 3)])
    anchor2 = lax.ppermute(anchor1, "x", [(1, 2)])

    parts = pl.pallas_call(
        question_kernel,
        out_shape=jax.ShapeDtypeStruct((NX * NT, 2 * HEADS, HEAD), bf16),
        in_specs=[SMEM, SMEM] + [VMEM] * 6,
        out_specs=VMEM,
        compiler_params=PARAMS,
        name="question",
    )(place, block_fill, asked, *others, near, far)

    parts = lax.all_to_all(parts, ("x", "tp"), 0, 0, tiled=True)

    block_output = pl.pallas_call(
        block_kernel,
        out_shape=jax.ShapeDtypeStruct(block_query.shape, bf16),
        in_specs=[SMEM, SMEM] + [VMEM] * 6,
        out_specs=VMEM,
        scratch_shapes=[pltpu.VMEM((2 * BLOCK, KVS * HEAD), bf16)],
        compiler_params=PARAMS,
        name="block",
    )(place, block_fill, block_query, unit, first, anchor1, anchor2, anchor3)

    question_output = pl.pallas_call(
        merge_kernel,
        out_shape=jax.ShapeDtypeStruct((1, NH * HEAD), bf16),
        in_specs=[VMEM],
        out_specs=VMEM,
        compiler_params=PARAMS,
        name="merge",
    )(parts)
    return block_output, question_output


def solution(mesh):
    fine = Mesh(mesh.devices.reshape(NX, NZ, NC, NT), ("x", "z", "core", "tp"))
    ctx = ("x", "z", "core")
    placed = P(ctx, "tp")
    return jax.shard_map(
        per_device,
        mesh=fine,
        in_specs=(placed,) * 6 + (P(),),
        out_specs=(placed, P(("x", "z", "core", "tp"), None)),
        check_vma=False,
    )
```

```python
import functools

import jax
import jax.numpy as jnp
from jax import lax
from jax.experimental import pallas as pl
from jax.experimental.pallas import tpu as pltpu
from jax.sharding import Mesh, PartitionSpec as P

NH = 64
KV_HEADS = 8
HEAD = 128
GROUPS = NH // KV_HEADS
BLOCK = 64
QTOK = 4
NX, NZ, NC, NT = 4, 8, 2, 4
HEADS = NH // NT
KVS = KV_HEADS // NT
UNIT = 144
SCALE = HEAD**-0.5
NEG = float("-inf")
ARRIVALS = ((0, 1), (1, 1), (0, 2), (1, 2), (0, 3), (1, 3), (0, 4))
X_FLIPS = (0, 1, 3, 2)
ROWS = NX * QTOK * GROUPS
SWAP = [(0, 1), (1, 0)]

VMEM = pl.BlockSpec(memory_space=pltpu.VMEM)
SMEM = pl.BlockSpec(memory_space=pltpu.SMEM)
PARAMS = pltpu.CompilerParams(vmem_limit_bytes=32 * 1024 * 1024)


def transpose_dot(left, right):
    return lax.dot_general(
        left, right, (((1,), (1,)), ((), ())), preferred_element_type=jnp.float32
    )


def arrived(place_ref, gatherer):
    x, z = place_ref[0], place_ref[1]
    blocks = []
    for crossed, steps in ARRIVALS:
        core = 1 - gatherer if crossed else gatherer
        at = lax.rem(z + NZ + jnp.where(gatherer == 0, -steps, steps), NZ)
        blocks.append(x * (NZ * NC) + at * NC + core)
    return blocks


def question_part(place_ref, fill_ref, asked_ref, others_ref, held, blocks):
    x, z, core = place_ref[0], place_ref[1], place_ref[2]
    count = len(blocks)
    context = count * BLOCK
    lane = lax.broadcasted_iota(jnp.int32, (1, context + count * 8), 1)
    is_tail = lane >= context
    tail_lane = lane - context
    owner = jnp.where(is_tail, tail_lane // 8, lane // BLOCK)
    offset = jnp.where(is_tail, tail_lane % 8, lane % BLOCK)
    fills = jnp.zeros_like(lane)
    first_ids = jnp.zeros_like(lane)
    for n, block in enumerate(blocks):
        fills = jnp.where(owner == n, fill_ref[block], fills)
        first_ids = jnp.where(owner == n, block * QTOK, first_ids)
    fills = jnp.where(is_tail, QTOK, fills)
    seen_from = jnp.where(is_tail, first_ids + offset, 0)
    seen_from = jnp.where(offset < fills, seen_from, 1 << 20)

    row = lax.broadcasted_iota(jnp.int32, (ROWS, 1), 0)
    row_ids = (row // GROUPS) % QTOK
    for n, flip in enumerate(X_FLIPS):
        first = ((x ^ flip) * (NZ * NC) + z * NC + core) * QTOK
        row_ids = jnp.where(row // (QTOK * GROUPS) == n, first + row_ids, row_ids)
    seen = seen_from <= row_ids

    queries = jnp.concatenate([asked_ref[...], others_ref[...].reshape(-1, HEADS, HEAD)], 0)
    queries = queries.astype(jnp.float32)
    tails = [ref[..., 2 * BLOCK : UNIT, :].astype(jnp.float32) for ref in held]
    tails = jnp.concatenate([t.reshape(-1, 16, KVS * HEAD) for t in tails], 0)
    tail_keys = tails[:, 0:8].reshape(count * 8, KVS * HEAD).astype(jnp.bfloat16)
    tail_values = tails[:, 8:16].reshape(count * 8, KVS * HEAD).astype(jnp.bfloat16)
    found = []
    for kv in range(KVS):
        cols = slice(kv * HEAD, (kv + 1) * HEAD)
        q = queries[:, kv * GROUPS : (kv + 1) * GROUPS, :].reshape(ROWS, HEAD).astype(jnp.bfloat16)
        keys = [ref[..., 0:BLOCK, cols].reshape(-1, HEAD) for ref in held]
        values = [ref[..., BLOCK : 2 * BLOCK, cols].reshape(-1, HEAD) for ref in held]
        keys = jnp.concatenate(keys + [tail_keys[:, cols]], 0)
        values = jnp.concatenate(values + [tail_values[:, cols]], 0)
        scores = jnp.where(seen, transpose_dot(q, keys) * SCALE, NEG)
        found.append((scores, jnp.max(scores, axis=1, keepdims=True), values))
    return found


def weigh(scores, peak, values):
    weights = jnp.exp(scores - peak).astype(jnp.bfloat16)
    total = jnp.sum(weights.astype(jnp.float32), axis=1, keepdims=True)
    return total, jnp.dot(weights, values, preferred_element_type=jnp.float32)


def rounded(array):
    return array.astype(jnp.bfloat16).astype(jnp.float32)


def near_kernel(
    place_ref, fill_ref, asked_ref, others_ref, unit_ref, swapped_ref, near_ref,
    peak_ref, total_ref, mixed_ref
):
    x, z, core = place_ref[0], place_ref[1], place_ref[2]
    own = x * (NZ * NC) + z * NC
    blocks = [own + core, own + 1 - core] + arrived(place_ref, core)
    held = (unit_ref, swapped_ref, near_ref)
    found = question_part(place_ref, fill_ref, asked_ref, others_ref, held, blocks)
    for kv, (scores, peak, values) in enumerate(found):
        peak = rounded(peak)
        total, mixed = weigh(scores, peak, values)
        peak_ref[kv] = jnp.broadcast_to(peak, (ROWS, HEAD))
        total_ref[kv] = jnp.broadcast_to(total, (ROWS, HEAD))
        mixed_ref[kv] = mixed


def far_kernel(
    place_ref, fill_ref, asked_ref, others_ref, far_ref, peak_ref, total_ref, mixed_ref, out_ref
):
    x, core = place_ref[0], place_ref[2]
    blocks = arrived(place_ref, 1 - core)
    found = question_part(place_ref, fill_ref, asked_ref, others_ref, (far_ref,), blocks)
    shape = (NX * QTOK, GROUPS, HEAD)
    outs, peaks, sums = [], [], []
    for kv, (scores, peak, values) in enumerate(found):
        old = peak_ref[kv]
        peak = rounded(jnp.maximum(peak, old[:, 0:1]))
        total, mixed = weigh(scores, peak, values)
        scale = jnp.exp(old - peak)
        outs.append((mixed + mixed_ref[kv] * scale).reshape(shape))
        peaks.append(jnp.broadcast_to(peak, (ROWS, HEAD)).reshape(shape))
        sums.append((total + total_ref[kv] * scale).reshape(shape))
    out = jnp.concatenate(outs, 1).astype(jnp.bfloat16)
    peak = jnp.concatenate(peaks, 1)
    total = jnp.concatenate(sums, 1)
    high = rounded(total)
    lane = lax.broadcasted_iota(jnp.int32, peak.shape, 2)
    stats = jnp.where(lane == 0, peak, jnp.where(lane == 1, high, jnp.where(lane == 2, total - high, 0.0)))
    stats = stats.astype(jnp.bfloat16)
    for n, flip in enumerate(X_FLIPS):
        target = pl.ds((x ^ flip) * QTOK, QTOK)
        out_ref[target, 0:HEADS, :] = out[n * QTOK : (n + 1) * QTOK]
        out_ref[target, HEADS : 2 * HEADS, :] = stats[n * QTOK : (n + 1) * QTOK]


def merge_kernel(parts_ref, out_ref):
    sums = parts_ref[:, 0:HEADS, :].astype(jnp.float32)
    stats = parts_ref[:, HEADS : 2 * HEADS, :].astype(jnp.float32)
    peaks = stats[:, :, 0:1]
    totals = stats[:, :, 1:2] + stats[:, :, 2:3]
    parts = [slice(x * NT, (x + 1) * NT) for x in range(NX)]
    top = functools.reduce(jnp.maximum, [peaks[p] for p in parts])
    scales = [jnp.exp(peaks[p] - top) for p in parts]
    num = sum(sums[p] * s for p, s in zip(parts, scales))
    den = sum(totals[p] * s for p, s in zip(parts, scales))
    result = num / den
    for t in range(NT):
        for h in range(HEADS):
            at = (t * HEADS + h) * HEAD
            out_ref[:, at : at + HEAD] = result[t, h : h + 1, :].astype(jnp.bfloat16)


def block_kernel(
    place_ref, fill_ref, query_ref, unit_ref, anchor_ref, out_ref
):
    x, z, core = place_ref[0], place_ref[1], place_ref[2]
    device = x * (NZ * NC) + z * NC + core
    row = lax.broadcasted_iota(jnp.int32, (BLOCK, 2 * BLOCK), 0)
    col = lax.broadcasted_iota(jnp.int32, (BLOCK, 2 * BLOCK), 1)
    own = col - BLOCK
    own_fill = fill_ref[device]
    anchor_fill = jnp.where(device > 0, fill_ref[0], 0)
    limit = jnp.where(col < BLOCK, anchor_fill, own_fill + BLOCK)
    allowed = (col < limit) & (own <= row)
    keep = lax.broadcasted_iota(jnp.int32, (BLOCK, 1), 0) < own_fill
    for kv in range(KVS):
        cols = slice(kv * HEAD, (kv + 1) * HEAD)
        keys = jnp.concatenate([anchor_ref[0:BLOCK, cols], unit_ref[0:BLOCK, cols]], 0)
        values = jnp.concatenate(
            [anchor_ref[BLOCK : 2 * BLOCK, cols], unit_ref[BLOCK : 2 * BLOCK, cols]], 0
        )
        heads = range(kv * GROUPS, (kv + 1) * GROUPS)
        q = jnp.concatenate([query_ref[:, h * HEAD : (h + 1) * HEAD] for h in heads], 0)
        scores = transpose_dot(q, keys) * SCALE
        scores = scores.reshape(GROUPS, BLOCK, 2 * BLOCK)
        scores = jnp.where(allowed[None], scores, NEG)
        peak = jnp.max(scores, axis=2, keepdims=True)
        weights = jnp.exp(scores - peak).astype(jnp.bfloat16)
        total = jnp.sum(weights.astype(jnp.float32), axis=2, keepdims=True)
        mixed = jnp.dot(
            weights.reshape(GROUPS * BLOCK, 2 * BLOCK), values, preferred_element_type=jnp.float32
        )
        mixed = mixed.reshape(GROUPS, BLOCK, HEAD) / total
        mixed = jnp.where(keep[None], mixed, 0.0).astype(jnp.bfloat16)
        for n, h in enumerate(heads):
            out_ref[:, h * HEAD : (h + 1) * HEAD] = mixed[n]


def flipped(array, flip):
    return lax.ppermute(array, "x", [(i, i ^ flip) for i in range(NX)])


def moved(array, steps):
    up = [(i * NC, (i + steps) % NZ * NC) for i in range(NZ)]
    down = [(i * NC + 1, (i - steps) % NZ * NC + 1) for i in range(NZ)]
    return lax.ppermute(array, ("z", "core"), up + down)


def per_device(
    block_query, block_key, block_value, question_query, question_key, question_value, block_fill
):
    bf16, f32 = jnp.bfloat16, jnp.float32
    x, z, core = lax.axis_index("x"), lax.axis_index("z"), lax.axis_index("core")
    place = jnp.stack([x, z, core]).astype(jnp.int32)

    gap = jnp.zeros((8 - QTOK, KVS * HEAD), bf16)
    unit = jnp.concatenate([block_key, block_value, question_key, gap, question_value, gap], 0)
    swapped = lax.ppermute(unit, "core", SWAP)
    pair = jnp.stack([unit, swapped])
    step1 = moved(pair, 1)
    step2 = moved(pair, 2)
    asked = question_query.reshape(QTOK, HEADS, HEAD)
    others = [flipped(asked, f) for f in X_FLIPS[1:]]
    step2, *others = lax.optimization_barrier((step2, *others))
    others = jnp.stack(others)
    step3 = moved(step2, 1)
    step4 = moved(step2[0], 2)
    near = jnp.concatenate([step1, step2, step3, step4[None]])
    far = lax.ppermute(near, "core", SWAP)

    rising = lax.dynamic_index_in_dim(
        jnp.where(core == 0, near, far), jnp.clip(2 * z - 2, 0, 6), 0, keepdims=False
    )
    falling = lax.dynamic_index_in_dim(
        jnp.where(core == 0, far, near), jnp.clip(2 * (NZ - z) - 1, 0, 6), 0, keepdims=False
    )
    here = jnp.where(core == 0, unit, swapped)
    first = jnp.where(z == 0, here, jnp.where(z <= NZ // 2, rising, falling))[: 2 * BLOCK]
    sent = lax.ppermute(first, ("x", "core"), [(0, NC), (1, 2 * NC + 1)])
    late = lax.ppermute(first, ("x", "core"), [(1, 3 * NC + 1)])

    question = functools.partial(pl.pallas_call, compiler_params=PARAMS)
    state = jax.ShapeDtypeStruct((KVS, ROWS, HEAD), f32)
    carry = question(
        near_kernel,
        out_shape=(state,) * 3,
        in_specs=[SMEM, SMEM] + [VMEM] * 5,
        out_specs=(VMEM,) * 3,
        cost_estimate=pl.CostEstimate(flops=10**8, bytes_accessed=10**6, transcendentals=10**5),
        name="question_near",
    )(place, block_fill, asked, others, unit, swapped, near)
    parts = question(
        far_kernel,
        out_shape=jax.ShapeDtypeStruct((NX * NT, 2 * HEADS, HEAD), bf16),
        in_specs=[SMEM, SMEM] + [VMEM] * 6,
        out_specs=VMEM,
        cost_estimate=pl.CostEstimate(flops=10**8, bytes_accessed=10**6, transcendentals=10**5),
        name="question_far",
    )(place, block_fill, asked, others, far, *carry)

    parts, sent, late = lax.optimization_barrier((parts, sent, late))
    got = jnp.where(x == NX - 1, late, sent)
    passed = lax.ppermute(got, ("x", "core"), [(2, 3), (5, 4), (7, 6)])
    receiver = jnp.where(x == 1, 0, 1)
    anchor = jnp.where(x == 0, first, jnp.where(core == receiver, got, passed))
    parts = lax.all_to_all(parts, ("x", "tp"), 0, 0, tiled=True)

    block_output = pl.pallas_call(
        block_kernel,
        out_shape=jax.ShapeDtypeStruct(block_query.shape, bf16),
        in_specs=[SMEM, SMEM] + [VMEM] * 3,
        out_specs=VMEM,
        compiler_params=PARAMS,
        name="block",
    )(place, block_fill, block_query, unit, anchor)

    question_output = pl.pallas_call(
        merge_kernel,
        out_shape=jax.ShapeDtypeStruct((1, NH * HEAD), bf16),
        in_specs=[VMEM],
        out_specs=VMEM,
        compiler_params=PARAMS,
        name="merge",
    )(parts)
    return block_output, question_output


def solution(mesh):
    fine = Mesh(mesh.devices.reshape(NX, NZ, NC, NT), ("x", "z", "core", "tp"))
    ctx = ("x", "z", "core")
    placed = P(ctx, "tp")
    return jax.shard_map(
        per_device,
        mesh=fine,
        in_specs=(placed,) * 6 + (P(),),
        out_specs=(placed, P(("x", "z", "core", "tp"), None)),
        check_vma=False,
    )
```

```python
import functools

import jax
import jax.numpy as jnp
from jax import lax
from jax.experimental import pallas as pl
from jax.experimental.pallas import tpu as pltpu
from jax.sharding import Mesh, PartitionSpec as P

NH = 64
KV_HEADS = 8
HEAD = 128
GROUPS = NH // KV_HEADS
BLOCK = 64
QTOK = 4
NX, NZ, NC, NT = 4, 8, 2, 4
HEADS = NH // NT
KVS = KV_HEADS // NT
UNIT = 144
SCALE = HEAD**-0.5
NEG = float("-inf")
ARRIVALS = ((0, 1), (1, 1), (0, 2), (1, 2), (0, 3), (1, 3), (0, 4))
X_FLIPS = (0, 2, 1, 3)
ROWS = NX * QTOK * GROUPS
SWAP = [(0, 1), (1, 0)]
GATHERED = len(ARRIVALS) * UNIT

VMEM = pl.BlockSpec(memory_space=pltpu.VMEM)
SMEM = pl.BlockSpec(memory_space=pltpu.SMEM)
PARAMS = pltpu.CompilerParams(vmem_limit_bytes=32 * 1024 * 1024)


def transpose_dot(left, right):
    return lax.dot_general(
        left, right, (((1,), (1,)), ((), ())), preferred_element_type=jnp.float32
    )


def arrived(place_ref, gatherer):
    x, z = place_ref[0], place_ref[1]
    blocks = []
    for crossed, steps in ARRIVALS:
        core = 1 - gatherer if crossed else gatherer
        at = lax.rem(z + NZ + jnp.where(gatherer == 0, -steps, steps), NZ)
        blocks.append(x * (NZ * NC) + at * NC + core)
    return blocks


def question_part(place_ref, fill_ref, asked_ref, others_ref, held, blocks):
    x, z, core = place_ref[0], place_ref[1], place_ref[2]
    count = len(blocks)
    context = count * BLOCK
    lane = lax.broadcasted_iota(jnp.int32, (1, context + count * 8), 1)
    is_tail = lane >= context
    tail_lane = lane - context
    owner = jnp.where(is_tail, tail_lane // 8, lane // BLOCK)
    offset = jnp.where(is_tail, tail_lane % 8, lane % BLOCK)
    fills = jnp.zeros_like(lane)
    first_ids = jnp.zeros_like(lane)
    for n, block in enumerate(blocks):
        fills = jnp.where(owner == n, fill_ref[block], fills)
        first_ids = jnp.where(owner == n, block * QTOK, first_ids)
    fills = jnp.where(is_tail, QTOK, fills)
    seen_from = jnp.where(is_tail, first_ids + offset, 0)
    seen_from = jnp.where(offset < fills, seen_from, 1 << 20)

    row = lax.broadcasted_iota(jnp.int32, (ROWS, 1), 0)
    row_ids = (row // GROUPS) % QTOK
    for n, flip in enumerate(X_FLIPS):
        first = ((x ^ flip) * (NZ * NC) + z * NC + core) * QTOK
        row_ids = jnp.where(row // (QTOK * GROUPS) == n, first + row_ids, row_ids)
    seen = seen_from <= row_ids

    queries = jnp.concatenate([asked_ref[...], others_ref[...].reshape(-1, HEADS, HEAD)], 0)
    queries = queries.astype(jnp.float32)
    tails = [ref[at + 2 * BLOCK : at + UNIT, :].astype(jnp.float32) for ref, at in held]
    tail_keys = jnp.concatenate([t[0:8] for t in tails], 0).astype(jnp.bfloat16)
    tail_values = jnp.concatenate([t[8:16] for t in tails], 0).astype(jnp.bfloat16)
    found = []
    for kv in range(KVS):
        cols = slice(kv * HEAD, (kv + 1) * HEAD)
        q = queries[:, kv * GROUPS : (kv + 1) * GROUPS, :].reshape(ROWS, HEAD).astype(jnp.bfloat16)
        keys = [ref[at : at + BLOCK, cols] for ref, at in held]
        values = [ref[at + BLOCK : at + 2 * BLOCK, cols] for ref, at in held]
        keys = jnp.concatenate(keys + [tail_keys[:, cols]], 0)
        values = jnp.concatenate(values + [tail_values[:, cols]], 0)
        scores = jnp.where(seen, transpose_dot(q, keys) * SCALE, NEG)
        found.append((scores, jnp.max(scores, axis=1, keepdims=True), values))
    return found


def weigh(scores, peak, values):
    weights = jnp.exp(scores - peak).astype(jnp.bfloat16)
    total = jnp.sum(weights.astype(jnp.float32), axis=1, keepdims=True)
    return total, jnp.dot(weights, values, preferred_element_type=jnp.float32)


def rounded(array):
    return array.astype(jnp.bfloat16).astype(jnp.float32)


def near_kernel(
    place_ref, fill_ref, asked_ref, others_ref, unit_ref, swapped_ref, near_ref,
    peak_ref, total_ref, mixed_ref
):
    x, z, core = place_ref[0], place_ref[1], place_ref[2]
    own = x * (NZ * NC) + z * NC
    blocks = [own + core, own + 1 - core] + arrived(place_ref, core)
    held = [(unit_ref, 0), (swapped_ref, 0)]
    held += [(near_ref, at) for at in range(0, GATHERED, UNIT)]
    found = question_part(place_ref, fill_ref, asked_ref, others_ref, held, blocks)
    for kv, (scores, peak, values) in enumerate(found):
        peak = rounded(peak)
        total, mixed = weigh(scores, peak, values)
        peak_ref[kv] = jnp.broadcast_to(peak, (ROWS, HEAD))
        total_ref[kv] = jnp.broadcast_to(total, (ROWS, HEAD))
        mixed_ref[kv] = mixed


def far_kernel(
    place_ref, fill_ref, asked_ref, others_ref, far_ref, peak_ref, total_ref, mixed_ref, out_ref
):
    x, core = place_ref[0], place_ref[2]
    blocks = arrived(place_ref, 1 - core)
    held = [(far_ref, at) for at in range(0, GATHERED, UNIT)]
    found = question_part(place_ref, fill_ref, asked_ref, others_ref, held, blocks)
    shape = (NX * QTOK, GROUPS, HEAD)
    outs, peaks, sums = [], [], []
    for kv, (scores, peak, values) in enumerate(found):
        old = peak_ref[kv]
        peak = rounded(jnp.maximum(peak, old[:, 0:1]))
        total, mixed = weigh(scores, peak, values)
        scale = jnp.exp(old - peak)
        outs.append((mixed + mixed_ref[kv] * scale).reshape(shape))
        peaks.append(jnp.broadcast_to(peak, (ROWS, HEAD)).reshape(shape))
        sums.append((total + total_ref[kv] * scale).reshape(shape))
    out = jnp.concatenate(outs, 1).astype(jnp.bfloat16)
    peak = jnp.concatenate(peaks, 1)
    total = jnp.concatenate(sums, 1)
    high = rounded(total)
    lane = lax.broadcasted_iota(jnp.int32, peak.shape, 2)
    stats = jnp.where(lane == 0, peak, jnp.where(lane == 1, high, jnp.where(lane == 2, total - high, 0.0)))
    stats = stats.astype(jnp.bfloat16)
    for n, flip in enumerate(X_FLIPS):
        target = pl.ds((x ^ flip) * QTOK, QTOK)
        out_ref[target, 0:HEADS, :] = out[n * QTOK : (n + 1) * QTOK]
        out_ref[target, HEADS : 2 * HEADS, :] = stats[n * QTOK : (n + 1) * QTOK]


def merge_kernel(parts_ref, out_ref):
    sums = parts_ref[:, 0:HEADS, :].astype(jnp.float32)
    stats = parts_ref[:, HEADS : 2 * HEADS, :].astype(jnp.float32)
    peaks = stats[:, :, 0:1]
    totals = stats[:, :, 1:2] + stats[:, :, 2:3]
    parts = [slice(x * NT, (x + 1) * NT) for x in range(NX)]
    top = functools.reduce(jnp.maximum, [peaks[p] for p in parts])
    scales = [jnp.exp(peaks[p] - top) for p in parts]
    num = sum(sums[p] * s for p, s in zip(parts, scales))
    den = sum(totals[p] * s for p, s in zip(parts, scales))
    result = num / den
    for t in range(NT):
        for h in range(HEADS):
            at = (t * HEADS + h) * HEAD
            out_ref[:, at : at + HEAD] = result[t, h : h + 1, :].astype(jnp.bfloat16)


def block_kernel(
    place_ref, fill_ref, query_ref, unit_ref, near_ref, far_ref, out_ref
):
    x, z, core = place_ref[0], place_ref[1], place_ref[2]
    device = x * (NZ * NC) + z * NC + core
    received = (z < NZ // 2) == (core == 0)
    row = lax.broadcasted_iota(jnp.int32, (BLOCK, 2 * BLOCK), 0)
    col = lax.broadcasted_iota(jnp.int32, (BLOCK, 2 * BLOCK), 1)
    own = col - BLOCK
    own_fill = fill_ref[device]
    anchor_fill = jnp.where(device > 0, fill_ref[0], 0)
    limit = jnp.where(col < BLOCK, anchor_fill, own_fill + BLOCK)
    allowed = (col < limit) & (own <= row)
    keep = lax.broadcasted_iota(jnp.int32, (BLOCK, 1), 0) < own_fill
    for kv in range(KVS):
        cols = slice(kv * HEAD, (kv + 1) * HEAD)
        anchor_rows = slice(GATHERED, GATHERED + 2 * BLOCK)
        anchor = jnp.where(received, near_ref[anchor_rows, cols], far_ref[anchor_rows, cols])
        keys = jnp.concatenate([anchor[0:BLOCK], unit_ref[0:BLOCK, cols]], 0)
        values = jnp.concatenate([anchor[BLOCK : 2 * BLOCK], unit_ref[BLOCK : 2 * BLOCK, cols]], 0)
        heads = range(kv * GROUPS, (kv + 1) * GROUPS)
        q = jnp.concatenate([query_ref[:, h * HEAD : (h + 1) * HEAD] for h in heads], 0)
        scores = transpose_dot(q, keys) * SCALE
        scores = scores.reshape(GROUPS, BLOCK, 2 * BLOCK)
        scores = jnp.where(allowed[None], scores, NEG)
        peak = jnp.max(scores, axis=2, keepdims=True)
        weights = jnp.exp(scores - peak).astype(jnp.bfloat16)
        total = jnp.sum(weights.astype(jnp.float32), axis=2, keepdims=True)
        mixed = jnp.dot(
            weights.reshape(GROUPS * BLOCK, 2 * BLOCK), values, preferred_element_type=jnp.float32
        )
        mixed = mixed.reshape(GROUPS, BLOCK, HEAD) / total
        mixed = jnp.where(keep[None], mixed, 0.0).astype(jnp.bfloat16)
        for n, h in enumerate(heads):
            out_ref[:, h * HEAD : (h + 1) * HEAD] = mixed[n]


def flipped(array, flip):
    return lax.ppermute(array, "x", [(i, i ^ flip) for i in range(NX)])


def moved(array, steps):
    up = [(i * NC, (i + steps) % NZ * NC) for i in range(NZ)]
    down = [(i * NC + 1, (i - steps) % NZ * NC + 1) for i in range(NZ)]
    return lax.ppermute(array, ("z", "core"), up + down)


def per_device(
    block_query, block_key, block_value, question_query, question_key, question_value, block_fill
):
    bf16, f32 = jnp.bfloat16, jnp.float32
    x, z, core = lax.axis_index("x"), lax.axis_index("z"), lax.axis_index("core")
    place = jnp.stack([x, z, core]).astype(jnp.int32)

    placed = (
        (block_key, 0),
        (block_value, BLOCK),
        (question_key, 2 * BLOCK),
        (question_value, 2 * BLOCK + 8),
    )
    unit = sum(jnp.pad(v, ((at, UNIT - at - v.shape[0]), (0, 0))) for v, at in placed)
    swapped = lax.ppermute(unit, "core", SWAP)
    pair = jnp.stack([unit, swapped])
    pair, question_query = lax.optimization_barrier((pair, question_query))
    asked = question_query.reshape(QTOK, HEADS, HEAD)
    step1 = moved(pair, 1)
    step2 = moved(pair, 2)
    first = jnp.where(core == 0, unit, swapped)[: 2 * BLOCK]
    third = lax.ppermute(first, ("x", "z", "core"), [(0, 3 * NC), (1, 5 * NC + 1)])
    fourth = lax.ppermute(first, ("x", "z", "core"), [(1, 4 * NC + 1)])

    step1, step2, third, fourth = lax.optimization_barrier((step1, step2, third, fourth))
    carried = jnp.where((z == 1) | (z == NZ - 1), jnp.where(core == 0, step1[0], step1[1]), unit)
    carried = jnp.where((z == 2) | (z == NZ - 2), jnp.where(core == 0, step2[0], step2[1]), carried)
    carried = carried[: 2 * BLOCK]
    carried = jnp.where((z == 3) | (z == 5), third, jnp.where(z == 4, fourth, carried))
    sent = jnp.concatenate([carried[:, :HEAD], carried[:, HEAD:], asked.reshape(-1, HEAD)], 0)
    step3 = moved(step2, 1)
    step4 = moved(step2[0], 2)
    came = [flipped(sent, f) for f in X_FLIPS[1:]]
    step3, step4, *came = lax.optimization_barrier((step3, step4, *came))
    near = jnp.concatenate([step1, step2, step3, step4[None]]).reshape(GATHERED, KVS * HEAD)
    others = jnp.stack([c[4 * BLOCK :] for c in came]).reshape(-1, HEADS, HEAD)
    anchor = sent
    for flip, c in zip(X_FLIPS[1:], came):
        anchor = jnp.where(x == flip, c, anchor)
    anchor = jnp.concatenate([anchor[: 2 * BLOCK], anchor[2 * BLOCK : 4 * BLOCK]], 1)
    near = jnp.concatenate([near, anchor], 0)
    far = lax.ppermute(near, "core", SWAP)

    question = functools.partial(pl.pallas_call, compiler_params=PARAMS)
    state = jax.ShapeDtypeStruct((KVS, ROWS, HEAD), f32)
    carry = question(
        near_kernel,
        out_shape=(state,) * 3,
        in_specs=[SMEM, SMEM] + [VMEM] * 5,
        out_specs=(VMEM,) * 3,
        cost_estimate=pl.CostEstimate(flops=10**8, bytes_accessed=10**6, transcendentals=10**5),
        name="question_near",
    )(place, block_fill, asked, others, unit, swapped, near)
    parts = question(
        far_kernel,
        out_shape=jax.ShapeDtypeStruct((NX * NT, 2 * HEADS, HEAD), bf16),
        in_specs=[SMEM, SMEM] + [VMEM] * 6,
        out_specs=VMEM,
        cost_estimate=pl.CostEstimate(flops=10**8, bytes_accessed=10**6, transcendentals=10**5),
        name="question_far",
    )(place, block_fill, asked, others, far, *carry)

    parts = lax.all_to_all(parts, ("x", "tp"), 0, 0, tiled=True)

    block_output = pl.pallas_call(
        block_kernel,
        out_shape=jax.ShapeDtypeStruct(block_query.shape, bf16),
        in_specs=[SMEM, SMEM] + [VMEM] * 4,
        out_specs=VMEM,
        compiler_params=PARAMS,
        name="block",
    )(place, block_fill, block_query, unit, near, far)

    question_output = pl.pallas_call(
        merge_kernel,
        out_shape=jax.ShapeDtypeStruct((1, NH * HEAD), bf16),
        in_specs=[VMEM],
        out_specs=VMEM,
        compiler_params=PARAMS,
        name="merge",
    )(parts)
    return block_output, question_output


def solution(mesh):
    fine = Mesh(mesh.devices.reshape(NX, NZ, NC, NT), ("x", "z", "core", "tp"))
    ctx = ("x", "z", "core")
    placed = P(ctx, "tp")
    return jax.shard_map(
        per_device,
        mesh=fine,
        in_specs=(placed,) * 6 + (P(),),
        out_specs=(placed, P(("x", "z", "core", "tp"), None)),
        check_vma=False,
    )
```

```python
import functools

import jax
import jax.numpy as jnp
from jax import lax
from jax.experimental import pallas as pl
from jax.experimental.pallas import tpu as pltpu
from jax.sharding import Mesh, PartitionSpec as P

NH = 64
KV_HEADS = 8
HEAD = 128
GROUPS = NH // KV_HEADS
BLOCK = 64
QTOK = 4
NX, NZ, NC, NT = 4, 8, 2, 4
HEADS = NH // NT
KVS = KV_HEADS // NT
UNIT = 144
SCALE = HEAD**-0.5
NEG = float("-inf")
ARRIVALS = ((0, 1), (1, 1), (0, 2), (1, 2), (0, 3), (1, 3), (0, 4))
X_FLIPS = (0, 2, 1, 3)
ROWS = NX * QTOK * GROUPS
SWAP = [(0, 1), (1, 0)]
GATHERED = len(ARRIVALS) * UNIT

VMEM = pl.BlockSpec(memory_space=pltpu.VMEM)
SMEM = pl.BlockSpec(memory_space=pltpu.SMEM)
PARAMS = pltpu.CompilerParams(vmem_limit_bytes=32 * 1024 * 1024)


def transpose_dot(left, right):
    return lax.dot_general(
        left, right, (((1,), (1,)), ((), ())), preferred_element_type=jnp.float32
    )


def arrived(place_ref, gatherer):
    x, z = place_ref[0], place_ref[1]
    blocks = []
    for crossed, steps in ARRIVALS:
        core = 1 - gatherer if crossed else gatherer
        at = lax.rem(z + NZ + jnp.where(gatherer == 0, -steps, steps), NZ)
        blocks.append(x * (NZ * NC) + at * NC + core)
    return blocks


def question_part(place_ref, fill_ref, asked_ref, others_ref, held, blocks):
    x, z, core = place_ref[0], place_ref[1], place_ref[2]
    count = len(blocks)
    context = count * BLOCK
    lane = lax.broadcasted_iota(jnp.int32, (1, context + count * 8), 1)
    is_tail = lane >= context
    tail_lane = lane - context
    owner = jnp.where(is_tail, tail_lane // 8, lane // BLOCK)
    offset = jnp.where(is_tail, tail_lane % 8, lane % BLOCK)
    fills = jnp.zeros_like(lane)
    first_ids = jnp.zeros_like(lane)
    for n, block in enumerate(blocks):
        fills = jnp.where(owner == n, fill_ref[block], fills)
        first_ids = jnp.where(owner == n, block * QTOK, first_ids)
    fills = jnp.where(is_tail, QTOK, fills)
    seen_from = jnp.where(is_tail, first_ids + offset, 0)
    seen_from = jnp.where(offset < fills, seen_from, 1 << 20)

    row = lax.broadcasted_iota(jnp.int32, (ROWS, 1), 0)
    row_ids = (row // GROUPS) % QTOK
    for n, flip in enumerate(X_FLIPS):
        first = ((x ^ flip) * (NZ * NC) + z * NC + core) * QTOK
        row_ids = jnp.where(row // (QTOK * GROUPS) == n, first + row_ids, row_ids)
    seen = seen_from <= row_ids

    queries = jnp.concatenate([asked_ref[...], others_ref[...].reshape(-1, HEADS, HEAD)], 0)
    queries = queries.astype(jnp.float32)
    tails = [ref[at + 2 * BLOCK : at + UNIT, :].astype(jnp.float32) for ref, at in held]
    tail_keys = jnp.concatenate([t[0:8] for t in tails], 0).astype(jnp.bfloat16)
    tail_values = jnp.concatenate([t[8:16] for t in tails], 0).astype(jnp.bfloat16)
    found = []
    for kv in range(KVS):
        cols = slice(kv * HEAD, (kv + 1) * HEAD)
        q = queries[:, kv * GROUPS : (kv + 1) * GROUPS, :].reshape(ROWS, HEAD).astype(jnp.bfloat16)
        keys = [ref[at : at + BLOCK, cols] for ref, at in held]
        values = [ref[at + BLOCK : at + 2 * BLOCK, cols] for ref, at in held]
        keys = jnp.concatenate(keys + [tail_keys[:, cols]], 0)
        values = jnp.concatenate(values + [tail_values[:, cols]], 0)
        scores = jnp.where(seen, transpose_dot(q, keys) * SCALE, NEG)
        found.append((scores, jnp.max(scores, axis=1, keepdims=True), values))
    return found


def weigh(scores, peak, values):
    weights = jnp.exp(scores - peak).astype(jnp.bfloat16)
    total = jnp.sum(weights.astype(jnp.float32), axis=1, keepdims=True)
    return total, jnp.dot(weights, values, preferred_element_type=jnp.float32)


def rounded(array):
    return array.astype(jnp.bfloat16).astype(jnp.float32)


def near_kernel(
    place_ref, fill_ref, asked_ref, others_ref, unit_ref, swapped_ref, near_ref,
    peak_ref, total_ref, mixed_ref
):
    x, z, core = place_ref[0], place_ref[1], place_ref[2]
    own = x * (NZ * NC) + z * NC
    blocks = [own + core, own + 1 - core] + arrived(place_ref, core)
    held = [(unit_ref, 0), (swapped_ref, 0)]
    held += [(near_ref, at) for at in range(0, GATHERED, UNIT)]
    found = question_part(place_ref, fill_ref, asked_ref, others_ref, held, blocks)
    for kv, (scores, peak, values) in enumerate(found):
        peak = rounded(peak)
        total, mixed = weigh(scores, peak, values)
        peak_ref[kv] = jnp.broadcast_to(peak, (ROWS, HEAD))
        total_ref[kv] = jnp.broadcast_to(total, (ROWS, HEAD))
        mixed_ref[kv] = mixed


def far_kernel(
    place_ref, fill_ref, asked_ref, others_ref, far_ref, peak_ref, total_ref, mixed_ref, out_ref
):
    x, core = place_ref[0], place_ref[2]
    blocks = arrived(place_ref, 1 - core)
    held = [(far_ref, at) for at in range(0, GATHERED, UNIT)]
    found = question_part(place_ref, fill_ref, asked_ref, others_ref, held, blocks)
    shape = (NX * QTOK, GROUPS, HEAD)
    outs, peaks, sums = [], [], []
    for kv, (scores, peak, values) in enumerate(found):
        old = peak_ref[kv]
        peak = rounded(jnp.maximum(peak, old[:, 0:1]))
        total, mixed = weigh(scores, peak, values)
        scale = jnp.exp(old - peak)
        outs.append((mixed + mixed_ref[kv] * scale).reshape(shape))
        peaks.append(jnp.broadcast_to(peak, (ROWS, HEAD)).reshape(shape))
        sums.append((total + total_ref[kv] * scale).reshape(shape))
    out = jnp.concatenate(outs, 1).astype(jnp.bfloat16)
    peak = jnp.concatenate(peaks, 1)
    total = jnp.concatenate(sums, 1)
    high = rounded(total)
    lane = lax.broadcasted_iota(jnp.int32, peak.shape, 2)
    stats = jnp.where(lane == 0, peak, jnp.where(lane == 1, high, jnp.where(lane == 2, total - high, 0.0)))
    stats = stats.astype(jnp.bfloat16)
    for n, flip in enumerate(X_FLIPS):
        target = pl.ds((x ^ flip) * QTOK, QTOK)
        out_ref[target, 0:HEADS, :] = out[n * QTOK : (n + 1) * QTOK]
        out_ref[target, HEADS : 2 * HEADS, :] = stats[n * QTOK : (n + 1) * QTOK]


def merge_kernel(parts_ref, out_ref):
    sums = parts_ref[:, 0:HEADS, :].astype(jnp.float32)
    stats = parts_ref[:, HEADS : 2 * HEADS, :].astype(jnp.float32)
    peaks = stats[:, :, 0:1]
    totals = stats[:, :, 1:2] + stats[:, :, 2:3]
    parts = [slice(x * NT, (x + 1) * NT) for x in range(NX)]
    top = functools.reduce(jnp.maximum, [peaks[p] for p in parts])
    scales = [jnp.exp(peaks[p] - top) for p in parts]
    num = sum(sums[p] * s for p, s in zip(parts, scales))
    den = sum(totals[p] * s for p, s in zip(parts, scales))
    result = num / den
    for t in range(NT):
        for h in range(HEADS):
            at = (t * HEADS + h) * HEAD
            out_ref[:, at : at + HEAD] = result[t, h : h + 1, :].astype(jnp.bfloat16)


def block_kernel(
    place_ref, fill_ref, query_ref, unit_ref, near_ref, far_ref, out_ref
):
    x, z, core = place_ref[0], place_ref[1], place_ref[2]
    device = x * (NZ * NC) + z * NC + core
    received = (z < NZ // 2) == (core == 0)
    row = lax.broadcasted_iota(jnp.int32, (BLOCK, 2 * BLOCK), 0)
    col = lax.broadcasted_iota(jnp.int32, (BLOCK, 2 * BLOCK), 1)
    own = col - BLOCK
    own_fill = fill_ref[device]
    anchor_fill = jnp.where(device > 0, fill_ref[0], 0)
    limit = jnp.where(col < BLOCK, anchor_fill, own_fill + BLOCK)
    allowed = (col < limit) & (own <= row)
    keep = lax.broadcasted_iota(jnp.int32, (BLOCK, 1), 0) < own_fill
    for kv in range(KVS):
        cols = slice(kv * HEAD, (kv + 1) * HEAD)
        anchor_rows = slice(GATHERED, GATHERED + 2 * BLOCK)
        anchor = jnp.where(received, near_ref[anchor_rows, cols], far_ref[anchor_rows, cols])
        keys = jnp.concatenate([anchor[0:BLOCK], unit_ref[0:BLOCK, cols]], 0)
        values = jnp.concatenate([anchor[BLOCK : 2 * BLOCK], unit_ref[BLOCK : 2 * BLOCK, cols]], 0)
        heads = range(kv * GROUPS, (kv + 1) * GROUPS)
        q = jnp.concatenate([query_ref[:, h * HEAD : (h + 1) * HEAD] for h in heads], 0)
        scores = transpose_dot(q, keys) * SCALE
        scores = scores.reshape(GROUPS, BLOCK, 2 * BLOCK)
        scores = jnp.where(allowed[None], scores, NEG)
        peak = jnp.max(scores, axis=2, keepdims=True)
        weights = jnp.exp(scores - peak).astype(jnp.bfloat16)
        total = jnp.sum(weights.astype(jnp.float32), axis=2, keepdims=True)
        mixed = jnp.dot(
            weights.reshape(GROUPS * BLOCK, 2 * BLOCK), values, preferred_element_type=jnp.float32
        )
        mixed = mixed.reshape(GROUPS, BLOCK, HEAD) / total
        mixed = jnp.where(keep[None], mixed, 0.0).astype(jnp.bfloat16)
        for n, h in enumerate(heads):
            out_ref[:, h * HEAD : (h + 1) * HEAD] = mixed[n]


def flipped(array, flip):
    return lax.ppermute(array, "x", [(i, i ^ flip) for i in range(NX)])


def moved(array, steps):
    up = [(i * NC, (i + steps) % NZ * NC) for i in range(NZ)]
    down = [(i * NC + 1, (i - steps) % NZ * NC + 1) for i in range(NZ)]
    return lax.ppermute(array, ("z", "core"), up + down)


def per_device(
    block_query, block_key, block_value, question_query, question_key, question_value, block_fill
):
    bf16, f32 = jnp.bfloat16, jnp.float32
    x, z, core = lax.axis_index("x"), lax.axis_index("z"), lax.axis_index("core")
    place = jnp.stack([x, z, core]).astype(jnp.int32)

    placed = (
        (block_key, 0),
        (block_value, BLOCK),
        (question_key, 2 * BLOCK),
        (question_value, 2 * BLOCK + 8),
    )
    unit = sum(jnp.pad(v, ((at, UNIT - at - v.shape[0]), (0, 0))) for v, at in placed)
    swapped = lax.ppermute(unit, "core", SWAP)
    pair = jnp.stack([unit, swapped])
    pair, question_query = lax.optimization_barrier((pair, question_query))
    asked = question_query.reshape(QTOK, HEADS, HEAD)
    step1 = moved(pair, 1)
    step2 = moved(unit, 2)
    first = jnp.where(core == 0, unit, swapped)[: 2 * BLOCK]
    third = lax.ppermute(first, ("x", "z", "core"), [(0, 3 * NC), (1, 5 * NC + 1)])
    fourth = lax.ppermute(first, ("x", "z", "core"), [(1, 4 * NC + 1), (0, 6 * NC + 1)])

    step1, step2 = lax.optimization_barrier((step1, step2))
    carried = jnp.where((z == 1) | (z == NZ - 1), jnp.where(core == 0, step1[0], step1[1]), unit)
    carried = jnp.where(z == 2, step2, carried)
    carried = carried[: 2 * BLOCK]
    carried = jnp.where((z == 3) | (z == 5), third, jnp.where((z == 4) | (z == 6), fourth, carried))
    sent = jnp.concatenate([carried[:, :HEAD], carried[:, HEAD:], asked.reshape(-1, HEAD)], 0)
    onward = jnp.stack([step1[1], step2])
    step3 = moved(onward, 1)
    step4 = moved(onward, 2)
    came = [flipped(sent, f) for f in X_FLIPS[1:]]
    step3, step4, *came = lax.optimization_barrier((step3, step4, *came))
    near = jnp.concatenate([step1, step2[None], step3, step4]).reshape(GATHERED, KVS * HEAD)
    others = jnp.stack([c[4 * BLOCK :] for c in came]).reshape(-1, HEADS, HEAD)
    anchor = sent
    for flip, c in zip(X_FLIPS[1:], came):
        anchor = jnp.where(x == flip, c, anchor)
    anchor = jnp.concatenate([anchor[: 2 * BLOCK], anchor[2 * BLOCK : 4 * BLOCK]], 1)
    near = jnp.concatenate([near, anchor], 0)
    far = lax.ppermute(near, "core", SWAP)

    question = functools.partial(pl.pallas_call, compiler_params=PARAMS)
    state = jax.ShapeDtypeStruct((KVS, ROWS, HEAD), f32)
    carry = question(
        near_kernel,
        out_shape=(state,) * 3,
        in_specs=[SMEM, SMEM] + [VMEM] * 5,
        out_specs=(VMEM,) * 3,
        cost_estimate=pl.CostEstimate(flops=10**8, bytes_accessed=10**6, transcendentals=10**5),
        name="question_near",
    )(place, block_fill, asked, others, unit, swapped, near)
    parts = question(
        far_kernel,
        out_shape=jax.ShapeDtypeStruct((NX * NT, 2 * HEADS, HEAD), bf16),
        in_specs=[SMEM, SMEM] + [VMEM] * 6,
        out_specs=VMEM,
        cost_estimate=pl.CostEstimate(flops=10**8, bytes_accessed=10**6, transcendentals=10**5),
        name="question_far",
    )(place, block_fill, asked, others, far, *carry)

    parts = lax.all_to_all(parts, ("x", "tp"), 0, 0, tiled=True)

    block_output = pl.pallas_call(
        block_kernel,
        out_shape=jax.ShapeDtypeStruct(block_query.shape, bf16),
        in_specs=[SMEM, SMEM] + [VMEM] * 4,
        out_specs=VMEM,
        compiler_params=PARAMS,
        name="block",
    )(place, block_fill, block_query, unit, near, far)

    question_output = pl.pallas_call(
        merge_kernel,
        out_shape=jax.ShapeDtypeStruct((1, NH * HEAD), bf16),
        in_specs=[VMEM],
        out_specs=VMEM,
        compiler_params=PARAMS,
        name="merge",
    )(parts)
    return block_output, question_output


def solution(mesh):
    fine = Mesh(mesh.devices.reshape(NX, NZ, NC, NT), ("x", "z", "core", "tp"))
    ctx = ("x", "z", "core")
    placed = P(ctx, "tp")
    return jax.shard_map(
        per_device,
        mesh=fine,
        in_specs=(placed,) * 6 + (P(),),
        out_specs=(placed, P(("x", "z", "core", "tp"), None)),
        check_vma=False,
    )
```

```python
import functools

import jax
import jax.numpy as jnp
from jax import lax
from jax.experimental import pallas as pl
from jax.experimental.pallas import tpu as pltpu
from jax.sharding import Mesh, PartitionSpec as P

NH = 64
KV_HEADS = 8
HEAD = 128
GROUPS = NH // KV_HEADS
BLOCK = 64
QTOK = 4
NX, NZ, NC, NT = 4, 8, 2, 4
HEADS = NH // NT
KVS = KV_HEADS // NT
UNIT = 144
SCALE = HEAD**-0.5
NEG = float("-inf")
ARRIVALS = ((0, 1), (1, 1), (0, 2), (1, 2), (0, 3), (1, 3), (0, 4))
X_FLIPS = (0, 2, 1, 3)
ROWS = NX * QTOK * GROUPS
SWAP = [(0, 1), (1, 0)]
GATHERED = len(ARRIVALS) * UNIT

VMEM = pl.BlockSpec(memory_space=pltpu.VMEM)
SMEM = pl.BlockSpec(memory_space=pltpu.SMEM)
PARAMS = pltpu.CompilerParams(vmem_limit_bytes=32 * 1024 * 1024)


def transpose_dot(left, right):
    return lax.dot_general(
        left, right, (((1,), (1,)), ((), ())), preferred_element_type=jnp.float32
    )


def arrived(place_ref, gatherer):
    x, z = place_ref[0], place_ref[1]
    blocks = []
    for crossed, steps in ARRIVALS:
        core = 1 - gatherer if crossed else gatherer
        at = lax.rem(z + NZ + jnp.where(gatherer == 0, -steps, steps), NZ)
        blocks.append(x * (NZ * NC) + at * NC + core)
    return blocks


def question_part(place_ref, fill_ref, asked_ref, others_ref, held, blocks):
    x, z, core = place_ref[0], place_ref[1], place_ref[2]
    count = len(blocks)
    context = count * BLOCK
    lane = lax.broadcasted_iota(jnp.int32, (1, context + count * 8), 1)
    is_tail = lane >= context
    tail_lane = lane - context
    owner = jnp.where(is_tail, tail_lane // 8, lane // BLOCK)
    offset = jnp.where(is_tail, tail_lane % 8, lane % BLOCK)
    fills = jnp.zeros_like(lane)
    first_ids = jnp.zeros_like(lane)
    for n, block in enumerate(blocks):
        fills = jnp.where(owner == n, fill_ref[block], fills)
        first_ids = jnp.where(owner == n, block * QTOK, first_ids)
    fills = jnp.where(is_tail, QTOK, fills)
    seen_from = jnp.where(is_tail, first_ids + offset, 0)
    seen_from = jnp.where(offset < fills, seen_from, 1 << 20)

    row = lax.broadcasted_iota(jnp.int32, (ROWS, 1), 0)
    row_ids = (row // GROUPS) % QTOK
    for n, flip in enumerate(X_FLIPS):
        first = ((x ^ flip) * (NZ * NC) + z * NC + core) * QTOK
        row_ids = jnp.where(row // (QTOK * GROUPS) == n, first + row_ids, row_ids)
    seen = seen_from <= row_ids

    queries = jnp.concatenate([asked_ref[...], others_ref[...].reshape(-1, HEADS, HEAD)], 0)
    queries = queries.astype(jnp.float32)
    tails = [ref[at + 2 * BLOCK : at + UNIT, :].astype(jnp.float32) for ref, at in held]
    tail_keys = jnp.concatenate([t[0:8] for t in tails], 0).astype(jnp.bfloat16)
    tail_values = jnp.concatenate([t[8:16] for t in tails], 0).astype(jnp.bfloat16)
    found = []
    for kv in range(KVS):
        cols = slice(kv * HEAD, (kv + 1) * HEAD)
        q = queries[:, kv * GROUPS : (kv + 1) * GROUPS, :].reshape(ROWS, HEAD).astype(jnp.bfloat16)
        keys = [ref[at : at + BLOCK, cols] for ref, at in held]
        values = [ref[at + BLOCK : at + 2 * BLOCK, cols] for ref, at in held]
        keys = jnp.concatenate(keys + [tail_keys[:, cols]], 0)
        values = jnp.concatenate(values + [tail_values[:, cols]], 0)
        scores = jnp.where(seen, transpose_dot(q, keys) * SCALE, NEG)
        found.append((scores, jnp.max(scores, axis=1, keepdims=True), values))
    return found


def weigh(scores, peak, values):
    weights = jnp.exp(scores - peak).astype(jnp.bfloat16)
    total = jnp.sum(weights.astype(jnp.float32), axis=1, keepdims=True)
    return total, jnp.dot(weights, values, preferred_element_type=jnp.float32)


def rounded(array):
    return array.astype(jnp.bfloat16).astype(jnp.float32)


def near_kernel(
    place_ref, fill_ref, asked_ref, others_ref, unit_ref, swapped_ref, near_ref,
    peak_ref, total_ref, mixed_ref
):
    x, z, core = place_ref[0], place_ref[1], place_ref[2]
    own = x * (NZ * NC) + z * NC
    blocks = [own + core, own + 1 - core] + arrived(place_ref, core)
    held = [(unit_ref, 0), (swapped_ref, 0)]
    held += [(near_ref, at) for at in range(0, GATHERED, UNIT)]
    found = question_part(place_ref, fill_ref, asked_ref, others_ref, held, blocks)
    for kv, (scores, peak, values) in enumerate(found):
        peak = rounded(peak)
        total, mixed = weigh(scores, peak, values)
        peak_ref[kv] = jnp.broadcast_to(peak, (ROWS, HEAD))
        total_ref[kv] = jnp.broadcast_to(total, (ROWS, HEAD))
        mixed_ref[kv] = mixed


def far_kernel(
    place_ref, fill_ref, asked_ref, others_ref, far_ref, peak_ref, total_ref, mixed_ref, out_ref
):
    x, core = place_ref[0], place_ref[2]
    blocks = arrived(place_ref, 1 - core)
    held = [(far_ref, at) for at in range(0, GATHERED, UNIT)]
    found = question_part(place_ref, fill_ref, asked_ref, others_ref, held, blocks)
    shape = (NX * QTOK, GROUPS, HEAD)
    outs, peaks, sums = [], [], []
    for kv, (scores, peak, values) in enumerate(found):
        old = peak_ref[kv]
        peak = rounded(jnp.maximum(peak, old[:, 0:1]))
        total, mixed = weigh(scores, peak, values)
        scale = jnp.exp(old - peak)
        outs.append((mixed + mixed_ref[kv] * scale).reshape(shape))
        peaks.append(jnp.broadcast_to(peak, (ROWS, HEAD)).reshape(shape))
        sums.append((total + total_ref[kv] * scale).reshape(shape))
    out = jnp.concatenate(outs, 1).astype(jnp.bfloat16)
    peak = jnp.concatenate(peaks, 1)
    total = jnp.concatenate(sums, 1)
    high = rounded(total)
    lane = lax.broadcasted_iota(jnp.int32, peak.shape, 2)
    stats = jnp.where(lane == 0, peak, jnp.where(lane == 1, high, jnp.where(lane == 2, total - high, 0.0)))
    stats = stats.astype(jnp.bfloat16)
    for n, flip in enumerate(X_FLIPS):
        target = pl.ds((x ^ flip) * QTOK, QTOK)
        out_ref[target, 0:HEADS, :] = out[n * QTOK : (n + 1) * QTOK]
        out_ref[target, HEADS : 2 * HEADS, :] = stats[n * QTOK : (n + 1) * QTOK]


def merge_kernel(parts_ref, out_ref):
    sums = parts_ref[:, 0:HEADS, :].astype(jnp.float32)
    stats = parts_ref[:, HEADS : 2 * HEADS, :].astype(jnp.float32)
    peaks = stats[:, :, 0:1]
    totals = stats[:, :, 1:2] + stats[:, :, 2:3]
    parts = [slice(x * NT, (x + 1) * NT) for x in range(NX)]
    top = functools.reduce(jnp.maximum, [peaks[p] for p in parts])
    scales = [jnp.exp(peaks[p] - top) for p in parts]
    num = sum(sums[p] * s for p, s in zip(parts, scales))
    den = sum(totals[p] * s for p, s in zip(parts, scales))
    result = num / den
    for t in range(NT):
        for h in range(HEADS):
            at = (t * HEADS + h) * HEAD
            out_ref[:, at : at + HEAD] = result[t, h : h + 1, :].astype(jnp.bfloat16)


def block_kernel(
    place_ref, fill_ref, query_ref, unit_ref, near_ref, far_ref, out_ref
):
    x, z, core = place_ref[0], place_ref[1], place_ref[2]
    device = x * (NZ * NC) + z * NC + core
    received = (z < NZ // 2) == (core == 0)
    row = lax.broadcasted_iota(jnp.int32, (BLOCK, 2 * BLOCK), 0)
    col = lax.broadcasted_iota(jnp.int32, (BLOCK, 2 * BLOCK), 1)
    own = col - BLOCK
    own_fill = fill_ref[device]
    anchor_fill = jnp.where(device > 0, fill_ref[0], 0)
    limit = jnp.where(col < BLOCK, anchor_fill, own_fill + BLOCK)
    allowed = (col < limit) & (own <= row)
    keep = lax.broadcasted_iota(jnp.int32, (BLOCK, 1), 0) < own_fill
    for kv in range(KVS):
        cols = slice(kv * HEAD, (kv + 1) * HEAD)
        anchor_rows = slice(GATHERED, GATHERED + 2 * BLOCK)
        anchor = jnp.where(received, near_ref[anchor_rows, cols], far_ref[anchor_rows, cols])
        keys = jnp.concatenate([anchor[0:BLOCK], unit_ref[0:BLOCK, cols]], 0)
        values = jnp.concatenate([anchor[BLOCK : 2 * BLOCK], unit_ref[BLOCK : 2 * BLOCK, cols]], 0)
        heads = range(kv * GROUPS, (kv + 1) * GROUPS)
        q = jnp.concatenate([query_ref[:, h * HEAD : (h + 1) * HEAD] for h in heads], 0)
        scores = transpose_dot(q, keys) * SCALE
        scores = scores.reshape(GROUPS, BLOCK, 2 * BLOCK)
        scores = jnp.where(allowed[None], scores, NEG)
        peak = jnp.max(scores, axis=2, keepdims=True)
        weights = jnp.exp(scores - peak).astype(jnp.bfloat16)
        total = jnp.sum(weights.astype(jnp.float32), axis=2, keepdims=True)
        mixed = jnp.dot(
            weights.reshape(GROUPS * BLOCK, 2 * BLOCK), values, preferred_element_type=jnp.float32
        )
        mixed = mixed.reshape(GROUPS, BLOCK, HEAD) / total
        mixed = jnp.where(keep[None], mixed, 0.0).astype(jnp.bfloat16)
        for n, h in enumerate(heads):
            out_ref[:, h * HEAD : (h + 1) * HEAD] = mixed[n]


def flipped(array, flip):
    return lax.ppermute(array, "x", [(i, i ^ flip) for i in range(NX)])


def moved(array, steps):
    up = [(i * NC, (i + steps) % NZ * NC) for i in range(NZ)]
    down = [(i * NC + 1, (i - steps) % NZ * NC + 1) for i in range(NZ)]
    return lax.ppermute(array, ("z", "core"), up + down)


def per_device(
    block_query, block_key, block_value, question_query, question_key, question_value, block_fill
):
    bf16, f32 = jnp.bfloat16, jnp.float32
    x, z, core = lax.axis_index("x"), lax.axis_index("z"), lax.axis_index("core")
    place = jnp.stack([x, z, core]).astype(jnp.int32)

    placed = (
        (block_key, 0),
        (block_value, BLOCK),
        (question_key, 2 * BLOCK),
        (question_value, 2 * BLOCK + 8),
    )
    unit = sum(jnp.pad(v, ((at, UNIT - at - v.shape[0]), (0, 0))) for v, at in placed)
    swapped = lax.ppermute(unit, "core", SWAP)
    pair = jnp.stack([unit, swapped])
    pair, question_query = lax.optimization_barrier((pair, question_query))
    asked = question_query.reshape(QTOK, HEADS, HEAD)
    step1 = moved(pair, 1)
    step2 = moved(unit, 2)
    first = jnp.where(core == 0, unit, swapped)[: 2 * BLOCK]
    third = lax.ppermute(first, ("x", "z", "core"), [(0, 3 * NC), (1, 5 * NC + 1)])
    fourth = lax.ppermute(first, ("x", "z", "core"), [(1, 4 * NC + 1), (0, 6 * NC + 1)])

    step1, step2 = lax.optimization_barrier((step1, step2))
    carried = jnp.where((z == 1) | (z == NZ - 1), jnp.where(core == 0, step1[0], step1[1]), unit)
    carried = jnp.where(z == 2, step2, carried)
    carried = carried[: 2 * BLOCK]
    carried = jnp.where((z == 3) | (z == 5), third, jnp.where((z == 4) | (z == 6), fourth, carried))
    sent = jnp.concatenate([carried[:, :HEAD], carried[:, HEAD:], asked.reshape(-1, HEAD)], 0)
    onward = jnp.stack([step1[1], step2])
    step3 = moved(onward, 1)
    step4 = moved(onward, 2)
    came = [flipped(sent, f) for f in X_FLIPS[1:]]
    near = jnp.concatenate([step1, step2[None], step3, step4]).reshape(GATHERED, KVS * HEAD)
    near, *came = lax.optimization_barrier((near, *came))
    others = jnp.stack([c[4 * BLOCK :] for c in came]).reshape(-1, HEADS, HEAD)
    anchor = sent
    for flip, c in zip(X_FLIPS[1:], came):
        anchor = jnp.where(x == flip, c, anchor)
    anchor = jnp.concatenate([anchor[: 2 * BLOCK], anchor[2 * BLOCK : 4 * BLOCK]], 1)
    near = jnp.concatenate([near, anchor], 0)
    far = lax.ppermute(near, "core", SWAP)

    question = functools.partial(pl.pallas_call, compiler_params=PARAMS)
    state = jax.ShapeDtypeStruct((KVS, ROWS, HEAD), f32)
    carry = question(
        near_kernel,
        out_shape=(state,) * 3,
        in_specs=[SMEM, SMEM] + [VMEM] * 5,
        out_specs=(VMEM,) * 3,
        cost_estimate=pl.CostEstimate(flops=10**8, bytes_accessed=10**6, transcendentals=10**5),
        name="question_near",
    )(place, block_fill, asked, others, unit, swapped, near)
    parts = question(
        far_kernel,
        out_shape=jax.ShapeDtypeStruct((NX * NT, 2 * HEADS, HEAD), bf16),
        in_specs=[SMEM, SMEM] + [VMEM] * 6,
        out_specs=VMEM,
        cost_estimate=pl.CostEstimate(flops=10**8, bytes_accessed=10**6, transcendentals=10**5),
        name="question_far",
    )(place, block_fill, asked, others, far, *carry)

    parts = lax.all_to_all(parts, ("x", "tp"), 0, 0, tiled=True)

    block_output = pl.pallas_call(
        block_kernel,
        out_shape=jax.ShapeDtypeStruct(block_query.shape, bf16),
        in_specs=[SMEM, SMEM] + [VMEM] * 4,
        out_specs=VMEM,
        compiler_params=PARAMS,
        name="block",
    )(place, block_fill, block_query, unit, near, far)

    question_output = pl.pallas_call(
        merge_kernel,
        out_shape=jax.ShapeDtypeStruct((1, NH * HEAD), bf16),
        in_specs=[VMEM],
        out_specs=VMEM,
        compiler_params=PARAMS,
        name="merge",
    )(parts)
    return block_output, question_output


def solution(mesh):
    fine = Mesh(mesh.devices.reshape(NX, NZ, NC, NT), ("x", "z", "core", "tp"))
    ctx = ("x", "z", "core")
    placed = P(ctx, "tp")
    return jax.shard_map(
        per_device,
        mesh=fine,
        in_specs=(placed,) * 6 + (P(),),
        out_specs=(placed, P(("x", "z", "core", "tp"), None)),
        check_vma=False,
    )
```

```python
import functools

import jax
import jax.numpy as jnp
from jax import lax
from jax.experimental import pallas as pl
from jax.experimental.pallas import tpu as pltpu
from jax.sharding import Mesh, PartitionSpec as P

NH = 64
KV_HEADS = 8
HEAD = 128
GROUPS = NH // KV_HEADS
BLOCK = 64
QTOK = 4
NX, NZ, NC, NT = 4, 8, 2, 4
HEADS = NH // NT
KVS = KV_HEADS // NT
UNIT = 144
SCALE = HEAD**-0.5
NEG = float("-inf")
ARRIVALS = ((0, 1), (1, 1), (0, 2), (1, 2), (0, 3), (1, 3), (0, 4))
X_FLIPS = (0, 2, 1, 3)
ROWS = NX * QTOK * GROUPS
SWAP = [(0, 1), (1, 0)]
GATHERED = len(ARRIVALS) * UNIT

VMEM = pl.BlockSpec(memory_space=pltpu.VMEM)
SMEM = pl.BlockSpec(memory_space=pltpu.SMEM)
PARAMS = pltpu.CompilerParams(vmem_limit_bytes=32 * 1024 * 1024)


def transpose_dot(left, right):
    return lax.dot_general(
        left, right, (((1,), (1,)), ((), ())), preferred_element_type=jnp.float32
    )


def arrived(place_ref, gatherer):
    x, z = place_ref[0], place_ref[1]
    blocks = []
    for crossed, steps in ARRIVALS:
        core = 1 - gatherer if crossed else gatherer
        at = lax.rem(z + NZ + jnp.where(gatherer == 0, -steps, steps), NZ)
        blocks.append(x * (NZ * NC) + at * NC + core)
    return blocks


def question_part(place_ref, fill_ref, asked_ref, others_ref, held, blocks):
    x, z, core = place_ref[0], place_ref[1], place_ref[2]
    count = len(blocks)
    context = count * BLOCK
    lane = lax.broadcasted_iota(jnp.int32, (1, context + count * 8), 1)
    is_tail = lane >= context
    tail_lane = lane - context
    owner = jnp.where(is_tail, tail_lane // 8, lane // BLOCK)
    offset = jnp.where(is_tail, tail_lane % 8, lane % BLOCK)
    fills = jnp.zeros_like(lane)
    first_ids = jnp.zeros_like(lane)
    for n, block in enumerate(blocks):
        fills = jnp.where(owner == n, fill_ref[block], fills)
        first_ids = jnp.where(owner == n, block * QTOK, first_ids)
    fills = jnp.where(is_tail, QTOK, fills)
    seen_from = jnp.where(is_tail, first_ids + offset, 0)
    seen_from = jnp.where(offset < fills, seen_from, 1 << 20)

    row = lax.broadcasted_iota(jnp.int32, (ROWS, 1), 0)
    row_ids = (row // GROUPS) % QTOK
    for n, flip in enumerate(X_FLIPS):
        first = ((x ^ flip) * (NZ * NC) + z * NC + core) * QTOK
        row_ids = jnp.where(row // (QTOK * GROUPS) == n, first + row_ids, row_ids)
    seen = seen_from <= row_ids

    queries = jnp.concatenate([asked_ref[...], others_ref[...].reshape(-1, HEADS, HEAD)], 0)
    queries = queries.astype(jnp.float32)
    tails = [ref[at + 2 * BLOCK : at + UNIT, :].astype(jnp.float32) for ref, at in held]
    tail_keys = jnp.concatenate([t[0:8] for t in tails], 0).astype(jnp.bfloat16)
    tail_values = jnp.concatenate([t[8:16] for t in tails], 0).astype(jnp.bfloat16)
    found = []
    for kv in range(KVS):
        cols = slice(kv * HEAD, (kv + 1) * HEAD)
        q = queries[:, kv * GROUPS : (kv + 1) * GROUPS, :].reshape(ROWS, HEAD).astype(jnp.bfloat16)
        keys = [ref[at : at + BLOCK, cols] for ref, at in held]
        values = [ref[at + BLOCK : at + 2 * BLOCK, cols] for ref, at in held]
        keys = jnp.concatenate(keys + [tail_keys[:, cols]], 0)
        values = jnp.concatenate(values + [tail_values[:, cols]], 0)
        scores = jnp.where(seen, transpose_dot(q, keys) * SCALE, NEG)
        found.append((scores, jnp.max(scores, axis=1, keepdims=True), values))
    return found


def weigh(scores, peak, values):
    weights = jnp.exp(scores - peak).astype(jnp.bfloat16)
    total = jnp.sum(weights.astype(jnp.float32), axis=1, keepdims=True)
    return total, jnp.dot(weights, values, preferred_element_type=jnp.float32)


def rounded(array):
    return array.astype(jnp.bfloat16).astype(jnp.float32)


def near_kernel(
    place_ref, fill_ref, asked_ref, others_ref, unit_ref, swapped_ref, near_ref,
    peak_ref, total_ref, mixed_ref
):
    x, z, core = place_ref[0], place_ref[1], place_ref[2]
    own = x * (NZ * NC) + z * NC
    blocks = [own + core, own + 1 - core] + arrived(place_ref, core)
    held = [(unit_ref, 0), (swapped_ref, 0)]
    held += [(near_ref, at) for at in range(0, GATHERED, UNIT)]
    found = question_part(place_ref, fill_ref, asked_ref, others_ref, held, blocks)
    for kv, (scores, peak, values) in enumerate(found):
        peak = rounded(peak)
        total, mixed = weigh(scores, peak, values)
        peak_ref[kv] = jnp.broadcast_to(peak, (ROWS, HEAD))
        total_ref[kv] = jnp.broadcast_to(total, (ROWS, HEAD))
        mixed_ref[kv] = mixed


def far_kernel(
    place_ref, fill_ref, asked_ref, others_ref, far_ref, peak_ref, total_ref, mixed_ref, out_ref
):
    x, core = place_ref[0], place_ref[2]
    blocks = arrived(place_ref, 1 - core)
    held = [(far_ref, at) for at in range(0, GATHERED, UNIT)]
    found = question_part(place_ref, fill_ref, asked_ref, others_ref, held, blocks)
    shape = (NX * QTOK, GROUPS, HEAD)
    outs, peaks, sums = [], [], []
    for kv, (scores, peak, values) in enumerate(found):
        old = peak_ref[kv]
        peak = rounded(jnp.maximum(peak, old[:, 0:1]))
        total, mixed = weigh(scores, peak, values)
        scale = jnp.exp(old - peak)
        outs.append((mixed + mixed_ref[kv] * scale).reshape(shape))
        peaks.append(jnp.broadcast_to(peak, (ROWS, HEAD)).reshape(shape))
        sums.append((total + total_ref[kv] * scale).reshape(shape))
    out = jnp.concatenate(outs, 1).astype(jnp.bfloat16)
    peak = jnp.concatenate(peaks, 1)
    total = jnp.concatenate(sums, 1)
    high = rounded(total)
    lane = lax.broadcasted_iota(jnp.int32, peak.shape, 2)
    stats = jnp.where(lane == 0, peak, jnp.where(lane == 1, high, jnp.where(lane == 2, total - high, 0.0)))
    stats = stats.astype(jnp.bfloat16)
    for n, flip in enumerate(X_FLIPS):
        target = pl.ds((x ^ flip) * QTOK, QTOK)
        out_ref[target, 0:HEADS, :] = out[n * QTOK : (n + 1) * QTOK]
        out_ref[target, HEADS : 2 * HEADS, :] = stats[n * QTOK : (n + 1) * QTOK]


def merge_kernel(parts_ref, out_ref):
    sums = parts_ref[:, 0:HEADS, :].astype(jnp.float32)
    stats = parts_ref[:, HEADS : 2 * HEADS, :].astype(jnp.float32)
    peaks = stats[:, :, 0:1]
    totals = stats[:, :, 1:2] + stats[:, :, 2:3]
    parts = [slice(x * NT, (x + 1) * NT) for x in range(NX)]
    top = functools.reduce(jnp.maximum, [peaks[p] for p in parts])
    scales = [jnp.exp(peaks[p] - top) for p in parts]
    num = sum(sums[p] * s for p, s in zip(parts, scales))
    den = sum(totals[p] * s for p, s in zip(parts, scales))
    result = num / den
    for t in range(NT):
        for h in range(HEADS):
            at = (t * HEADS + h) * HEAD
            out_ref[:, at : at + HEAD] = result[t, h : h + 1, :].astype(jnp.bfloat16)


def block_kernel(
    place_ref, fill_ref, query_ref, unit_ref, near_ref, far_ref, out_ref
):
    x, z, core = place_ref[0], place_ref[1], place_ref[2]
    device = x * (NZ * NC) + z * NC + core
    received = (z < NZ // 2) == (core == 0)
    row = lax.broadcasted_iota(jnp.int32, (BLOCK, 2 * BLOCK), 0)
    col = lax.broadcasted_iota(jnp.int32, (BLOCK, 2 * BLOCK), 1)
    own = col - BLOCK
    own_fill = fill_ref[device]
    anchor_fill = jnp.where(device > 0, fill_ref[0], 0)
    limit = jnp.where(col < BLOCK, anchor_fill, own_fill + BLOCK)
    allowed = (col < limit) & (own <= row)
    keep = lax.broadcasted_iota(jnp.int32, (BLOCK, 1), 0) < own_fill
    for kv in range(KVS):
        cols = slice(kv * HEAD, (kv + 1) * HEAD)
        anchor_rows = slice(GATHERED, GATHERED + 2 * BLOCK)
        anchor = jnp.where(received, near_ref[anchor_rows, cols], far_ref[anchor_rows, cols])
        keys = jnp.concatenate([anchor[0:BLOCK], unit_ref[0:BLOCK, cols]], 0)
        values = jnp.concatenate([anchor[BLOCK : 2 * BLOCK], unit_ref[BLOCK : 2 * BLOCK, cols]], 0)
        heads = range(kv * GROUPS, (kv + 1) * GROUPS)
        q = jnp.concatenate([query_ref[:, h * HEAD : (h + 1) * HEAD] for h in heads], 0)
        scores = transpose_dot(q, keys) * SCALE
        scores = scores.reshape(GROUPS, BLOCK, 2 * BLOCK)
        scores = jnp.where(allowed[None], scores, NEG)
        peak = jnp.max(scores, axis=2, keepdims=True)
        weights = jnp.exp(scores - peak).astype(jnp.bfloat16)
        total = jnp.sum(weights.astype(jnp.float32), axis=2, keepdims=True)
        mixed = jnp.dot(
            weights.reshape(GROUPS * BLOCK, 2 * BLOCK), values, preferred_element_type=jnp.float32
        )
        mixed = mixed.reshape(GROUPS, BLOCK, HEAD) / total
        mixed = jnp.where(keep[None], mixed, 0.0).astype(jnp.bfloat16)
        for n, h in enumerate(heads):
            out_ref[:, h * HEAD : (h + 1) * HEAD] = mixed[n]


def flipped(array, flip):
    return lax.ppermute(array, "x", [(i, i ^ flip) for i in range(NX)])


def moved(array, steps):
    up = [(i * NC, (i + steps) % NZ * NC) for i in range(NZ)]
    down = [(i * NC + 1, (i - steps) % NZ * NC + 1) for i in range(NZ)]
    return lax.ppermute(array, ("z", "core"), up + down)


def per_device(
    block_query, block_key, block_value, question_query, question_key, question_value, block_fill
):
    bf16, f32 = jnp.bfloat16, jnp.float32
    x, z, core = lax.axis_index("x"), lax.axis_index("z"), lax.axis_index("core")
    place = jnp.stack([x, z, core]).astype(jnp.int32)

    placed = (
        (block_key, 0),
        (block_value, BLOCK),
        (question_key, 2 * BLOCK),
        (question_value, 2 * BLOCK + 8),
    )
    unit = sum(jnp.pad(v, ((at, UNIT - at - v.shape[0]), (0, 0))) for v, at in placed)
    swapped = lax.ppermute(unit, "core", SWAP)
    pair = jnp.stack([unit, swapped])
    pair, question_query = lax.optimization_barrier((pair, question_query))
    asked = question_query.reshape(QTOK, HEADS, HEAD)
    step1 = moved(pair, 1)
    step2 = moved(unit, 2)
    first = jnp.where(core == 0, unit, swapped)[: 2 * BLOCK]
    third = lax.ppermute(first, ("x", "z", "core"), [(1, 4 * NC + 1), (0, 6 * NC + 1)])
    fourth = lax.ppermute(first, ("x", "z", "core"), [(0, 3 * NC), (1, 5 * NC + 1)])

    step1, step2 = lax.optimization_barrier((step1, step2))
    carried = jnp.where((z == 1) | (z == NZ - 1), jnp.where(core == 0, step1[0], step1[1]), unit)
    carried = jnp.where(z == 2, step2, carried)
    carried = carried[: 2 * BLOCK]
    carried = jnp.where((z == 4) | (z == 6), third, jnp.where((z == 3) | (z == 5), fourth, carried))
    sent = jnp.concatenate([carried[:, :HEAD], carried[:, HEAD:], asked.reshape(-1, HEAD)], 0)
    onward = jnp.stack([step1[1], step2])
    step3 = moved(onward, 1)
    step4 = moved(onward, 2)
    came = [flipped(sent, f) for f in X_FLIPS[1:]]
    step3, step4, *came = lax.optimization_barrier((step3, step4, *came))
    near = jnp.concatenate([step1, step2[None], step3, step4]).reshape(GATHERED, KVS * HEAD)
    others = jnp.stack([c[4 * BLOCK :] for c in came]).reshape(-1, HEADS, HEAD)
    anchor = sent
    for flip, c in zip(X_FLIPS[1:], came):
        anchor = jnp.where(x == flip, c, anchor)
    anchor = jnp.concatenate([anchor[: 2 * BLOCK], anchor[2 * BLOCK : 4 * BLOCK]], 1)
    near = jnp.concatenate([near, anchor], 0)
    far = lax.ppermute(near, "core", SWAP)

    question = functools.partial(pl.pallas_call, compiler_params=PARAMS)
    state = jax.ShapeDtypeStruct((KVS, ROWS, HEAD), f32)
    carry = question(
        near_kernel,
        out_shape=(state,) * 3,
        in_specs=[SMEM, SMEM] + [VMEM] * 5,
        out_specs=(VMEM,) * 3,
        cost_estimate=pl.CostEstimate(flops=10**8, bytes_accessed=10**6, transcendentals=10**5),
        name="question_near",
    )(place, block_fill, asked, others, unit, swapped, near)
    parts = question(
        far_kernel,
        out_shape=jax.ShapeDtypeStruct((NX * NT, 2 * HEADS, HEAD), bf16),
        in_specs=[SMEM, SMEM] + [VMEM] * 6,
        out_specs=VMEM,
        cost_estimate=pl.CostEstimate(flops=10**8, bytes_accessed=10**6, transcendentals=10**5),
        name="question_far",
    )(place, block_fill, asked, others, far, *carry)

    parts = lax.all_to_all(parts, ("x", "tp"), 0, 0, tiled=True)

    block_output = pl.pallas_call(
        block_kernel,
        out_shape=jax.ShapeDtypeStruct(block_query.shape, bf16),
        in_specs=[SMEM, SMEM] + [VMEM] * 4,
        out_specs=VMEM,
        compiler_params=PARAMS,
        name="block",
    )(place, block_fill, block_query, unit, near, far)

    question_output = pl.pallas_call(
        merge_kernel,
        out_shape=jax.ShapeDtypeStruct((1, NH * HEAD), bf16),
        in_specs=[VMEM],
        out_specs=VMEM,
        compiler_params=PARAMS,
        name="merge",
    )(parts)
    return block_output, question_output


def solution(mesh):
    fine = Mesh(mesh.devices.reshape(NX, NZ, NC, NT), ("x", "z", "core", "tp"))
    ctx = ("x", "z", "core")
    placed = P(ctx, "tp")
    return jax.shard_map(
        per_device,
        mesh=fine,
        in_specs=(placed,) * 6 + (P(),),
        out_specs=(placed, P(("x", "z", "core", "tp"), None)),
        check_vma=False,
    )
```
